128 devices in a mesh: row: 8 (over z, core), col: 16 (over y, x).
Axes of the slice: x: 4, y: 4, z: 4, core: 2. Of those that a mesh axis runs over, the one named last changes fastest.
Arguments:
- density: float32 [6144, 6144], P('row', 'col'), as said below
- keep_mask: int32 [48, 48], replicated, may hold values from 0 to 1, as said below
- owner_map: int32 [48], replicated, may hold values from 0 to 7, as said below
Outputs:
- owned_density: float32 [8192, 6144], P('row', 'col')
The draws below stay inside these ranges and needn't reach their ends.
Inputs may be any that keep to these rules, and one draw needn't show every extreme that they name: density is symmetric. `keep_mask`: symmetric, with ones on the diagonal. `owner_map`: each owner has between 4 and 8 block rows, and 8 is reached; of the 6 block rows k * 6 to k * 6 + 5 at most 2 have one owner, and 2 is reached.
All inputs are finite; a program needn't handle non-finite values.
Results may differ from the reference program's by a relative error of at most 0.0051.
Values may be sent and summed in bfloat16 or wider, within the bound.
A program may use at most 64 MiB of HBM per device.

```python
import math
import jax
import jax.numpy as jnp

BS = 128
STEPS = 1
NB = 48
NBR = 6
CAPR = 8
NORB = 6144
NOCC = 3072
N_ROW = 8


def draw_density(key, part):
    base_key = jax.random.fold_in(key, 11)
    key_matrix, key_jitter, key_slabs = jax.random.split(base_key, 3)
    order_total = NB * BS
    groups = NB // NBR
    samples = jax.random.normal(key_matrix, (order_total, order_total), jnp.float32)
    coupling_size = 0.5
    low_level = 0.1
    high_level = 0.7
    spread_scale = coupling_size / math.sqrt(order_total)
    coupling = (samples + samples.T) * (0.70710678 * spread_scale)
    slab_rank = jax.random.permutation(key_slabs, groups).astype(jnp.float32)
    slab_level = 0.15 + 0.7 * slab_rank / (groups - 1)
    orbital_slab = jnp.arange(order_total) // (NBR * BS)
    jitter = jax.random.uniform(key_jitter, (order_total,), jnp.float32, -0.15, 0.15)
    fraction = slab_level[orbital_slab] + jitter
    levels = low_level + (high_level - low_level) * fraction
    return coupling + jnp.diag(levels)


def draw_keep_mask(key, part):
    levels = jax.random.randint(jax.random.fold_in(key, 23), (NB, NB), 0, 5)
    kept_blocks = (levels < 1).astype(jnp.int32)
    upper_part = jnp.arange(NB)[:, None] <= jnp.arange(NB)[None, :]
    mirrored = jnp.where(upper_part, kept_blocks, kept_blocks.T)
    return jnp.where(jnp.eye(NB, dtype=bool), 1, mirrored).astype(jnp.int32)


def draw_owner_map(key, part):
    key_rotate, key_labels, key_order = jax.random.split(jax.random.fold_in(key, 37), 3)
    groups = NB // NBR
    slab_ids = jnp.arange(groups)[:, None]
    position = jnp.arange(NBR)[None, :]
    destination = (slab_ids + position) % groups
    first_owner = jax.random.randint(key_rotate, (), 0, groups)
    before_owner = (first_owner - 1 + groups) % groups
    moved = (slab_ids == first_owner) & (position == 1) | (slab_ids == before_owner) & (position == 2)
    destination = jnp.where(moved, first_owner, destination)
    relabel = jax.random.permutation(key_labels, groups)
    destination = relabel[destination]
    sort_keys = jax.random.randint(key_order, (groups, NBR), 0, 1 << 20) * NBR + position
    ordering = jnp.argsort(sort_keys, axis=1)
    destination = jnp.take_along_axis(destination, ordering, axis=1)
    return destination.reshape(NB).astype(jnp.int32)


def setup_inputs(seed: int = 0) -> dict:
    streams_of = jax.random.split(jax.random.key(seed), 4)
    return {
        "density": draw_density(jax.random.fold_in(streams_of[3], 71), 0),
        "keep_mask": draw_keep_mask(jax.random.fold_in(streams_of[3], 71), 0),
        "owner_map": draw_owner_map(jax.random.fold_in(streams_of[3], 71), 0),
    }


def expand_mask(keep_mask):
    weights = keep_mask.astype(jnp.float32)
    return jnp.repeat(jnp.repeat(weights, BS, axis=0), BS, axis=1)


def reference(density, keep_mask, owner_map):
    keep_full = expand_mask(keep_mask)
    current = density * keep_full
    for sweep_index in range(STEPS):
        current_half = current.astype(jnp.bfloat16)
        square = keep_full * jnp.dot(current_half, current_half, preferred_element_type=jnp.float32)
        square_half = square.astype(jnp.bfloat16)
        cubic_term = jnp.dot(square_half, current_half, preferred_element_type=jnp.float32)
        quartic = jnp.dot(square_half, square_half, preferred_element_type=jnp.float32)
        difference = current - square
        spread = jnp.sum(difference * difference)
        filling = 4.0 * jnp.trace(cubic_term) - 3.0 * jnp.trace(quartic)
        factor = (jnp.float32(NOCC) - filling) / (spread + 1e-6)
        current = keep_full * (4.0 * cubic_term - 3.0 * quartic + factor * (square - 2.0 * cubic_term + quartic))
    positions = jnp.arange(NB).astype(jnp.int32)
    same_owner = owner_map[:, None] == owner_map[None, :]
    earlier = positions[None, :] < positions[:, None]
    ranking = jnp.sum(same_owner & earlier, axis=1).astype(jnp.int32)
    target_slot = (owner_map * CAPR + ranking).astype(jnp.int32)
    block_rows = current.reshape(NB, BS, NORB)
    owned_rows = jnp.zeros((N_ROW * CAPR, BS, NORB), jnp.float32).at[target_slot].set(block_rows)
    return owned_rows.reshape(N_ROW * CAPR * BS, NORB)
```

```python
import jax
import jax.numpy as jnp
from jax import lax
from jax.experimental import pallas as pl
from jax.experimental.pallas import tpu as pltpu
from jax.sharding import PartitionSpec as P

MESH = pl.DeviceIdType.MESH
F32 = jnp.float32
BF16 = jnp.bfloat16


def kernel(
    dens, keep, owner, out,
    row_c, row_s, col_c, col_s, square, cubic, quartic, moved, sums, sums_in,
    send_sem, row_sem, col_sem, sib_sem, end_sem, end_sib_sem, sum_sem,
):
    rows, cols = dens.shape
    half = rows // 2
    r = lax.axis_index("row")
    c = lax.axis_index("col")
    z, p = r // 2, r % 2
    y, x = c // 4, c % 4
    sign = 1 - 2 * p
    bs = cols // 3
    per = rows // bs

    def at(dz=0, dp=0, dy=0, dx=0):
        return (
            lax.rem(z + dz + 4, 4) * 2 + lax.rem(p + dp, 2),
            lax.rem(y + dy + 4, 4) * 4 + lax.rem(x + dx + 4, 4),
        )

    peers = {}
    for k in (1, 2, 3):
        peers["x", k], peers["y", k], peers["z", k] = at(dx=k), at(dy=k), at(dz=k)
    peers["p", 1] = at(dp=1)
    fwd = {"x": at(dx=sign), "y": at(dy=sign), "z": at(dz=sign)}
    bwd = {"x": at(dx=-sign), "y": at(dy=-sign), "z": at(dz=-sign)}

    barrier = pltpu.get_barrier_semaphore()
    for device in peers.values():
        pl.semaphore_signal(barrier, inc=1, device_id=device, device_id_type=MESH)

    def block(i, j):
        return (slice(i * bs, (i + 1) * bs), slice(j * bs, (j + 1) * bs))

    def kept(i, j):
        return keep[r * per + i, c * 3 + j].astype(F32)

    for i in range(per):
        for j in range(3):
            value = (dens[block(i, j)] * kept(i, j)).astype(BF16)
            h, i2 = divmod(i, per // 2)
            row_c[(h, 0) + block(i2, j)] = value
            col_c[(2 * r + h,) + block(i2, j)] = value

    pl.semaphore_wait(barrier, len(peers))

    started = []

    def send(src, dst, recv, device):
        copy = pltpu.make_async_remote_copy(
            src_ref=src, dst_ref=dst, send_sem=send_sem.at[len(started)],
            recv_sem=recv, device_id=device, device_id_type=MESH,
        )
        copy.start()
        started.append(copy)

    def arrived(dst, recv):
        pltpu.make_async_remote_copy(
            src_ref=dst, dst_ref=dst, send_sem=send_sem.at[0],
            recv_sem=recv, device_id=peers["p", 1], device_id_type=MESH,
        ).wait_recv()

    def slot(h, first, second):
        return 4 * second + first if h == 0 else 4 * first + second

    def gather(stage, row, col, product, on_round):
        routes = (("x", "y"), ("y", "x"))

        def pass_on(h, first, second, which, direction):
            step = 1 if direction is fwd else 3
            there = ((first + step) % 4, second) if which == 0 else (first, (second + step) % 4)
            goal = slot(h, *there)
            send(
                row.at[h, slot(h, first, second)], row.at[h, goal],
                row_sem.at[stage, h, goal], direction[routes[h][which]],
            )

        def have(h, first, second):
            if second == 0:
                if first == 0:
                    pass_on(h, 0, 0, 0, fwd)
                    pass_on(h, 0, 0, 0, bwd)
                    return
                if first == 1:
                    pass_on(h, 1, 0, 0, fwd)
                second_stage(h, first)
            elif second == 1:
                pass_on(h, first, 1, 1, fwd)

        def second_stage(h, first):
            pass_on(h, first, 0, 1, fwd)
            pass_on(h, first, 0, 1, bwd)

        def columns(core, away, lane_sign):
            source = lax.rem(z - lane_sign * away + 8, 4) * 2 + core
            return col.at[pl.ds(2 * source, 2)]

        def have_col(away):
            piece = columns(p, away, sign)
            for step, direction in ((1, fwd), (3, bwd)):
                if away == 0 or (away == 1 and step == 1):
                    send(piece, piece, col_sem.at[stage, (away + step) % 4], direction["z"])
            send(piece, piece, sib_sem.at[stage, away], peers["p", 1])

        waiting = []

        def multiply(count):
            for _ in range(min(count, len(waiting))):
                h, first, second = waiting.pop(0)
                place = slot(h, first, second)
                behind_y, behind_x = divmod(place, 4)
                k = lax.rem(y - sign * behind_y + 8, 4) * 4 + lax.rem(x - sign * behind_x + 8, 4)
                product(h, row.at[h, place], k)

        for h in range(2):
            have(h, 0, 0)
        have_col(0)
        for h in range(2):
            second_stage(h, 0)
        waiting += [(0, 0, 0), (1, 0, 0)]
        order = (
            ((1, 0), (3, 0)),
            ((0, 1), (0, 3)),
            ((2, 0),),
            ((1, 1), (3, 1), (1, 3), (3, 3)),
            ((0, 2), (2, 1), (2, 3)),
            ((1, 2), (3, 2)),
            ((2, 2),),
        )
        for number, pieces in enumerate(order):
            for first, second in pieces:
                for h in range(2):
                    place = slot(h, first, second)
                    arrived(row.at[h, place], row_sem.at[stage, h, place])
                    have(h, first, second)
                    waiting.append((h, first, second))
                    if number > 2:
                        multiply(2)
                if number in (0, 2):
                    arrived(columns(p, first, sign), col_sem.at[stage, first])
                    have_col(first)
            if number == 2:
                for away in range(4):
                    arrived(columns(1 - p, away, -sign), sib_sem.at[stage, away])
            on_round(number)
        multiply(len(waiting))

    def add(total, h, a, b):
        here = pl.ds(h * half, half)
        total[here, :] += jnp.dot(a[...], b, preferred_element_type=F32)

    def first_product(h, piece, k):
        add(square, h, piece, col_c[k])

    def second_product(h, piece, k):
        add(cubic, h, piece, col_c[k])
        add(quartic, h, piece, col_s[k])

    square[...] = jnp.zeros_like(square)
    cubic[...] = jnp.zeros_like(cubic)
    quartic[...] = jnp.zeros_like(quartic)

    gather(0, row_c, col_c, first_product, lambda number: None)

    fold = lambda v: jnp.sum(v.reshape(bs // 8, 8, bs), axis=0)
    totals = [jnp.zeros((8, bs), F32)] * 3
    for i in range(per):
        for j in range(3):
            mask = kept(i, j)
            value = square[block(i, j)] * mask
            square[block(i, j)] = value
            rounded = value.astype(BF16)
            h, i2 = divmod(i, per // 2)
            row_s[(h, 0) + block(i2, j)] = rounded
            col_s[(2 * r + h,) + block(i2, j)] = rounded
            difference = dens[block(i, j)] * mask - value
            wide = rounded.astype(F32)
            one = row_c[(h, 0) + block(i2, j)].astype(F32)
            terms = (wide * one, wide * wide, difference * difference)
            totals = [t + fold(v) for t, v in zip(totals, terms, strict=True)]
    for n in range(3):
        sums[0, n] = totals[n]

    def reduce_start(step, axis, count):
        for k in range(1, count):
            send(sums.at[step], sums_in.at[step, k - 1], sum_sem.at[step, k - 1], peers[axis, k])

    def reduce_end(step, count):
        total = sums[step]
        for k in range(1, count):
            arrived(sums_in.at[step, k - 1], sum_sem.at[step, k - 1])
            total += sums_in[step, k - 1]
        sums[step + 1] = total

    axes = (("z", 4), ("p", 2), ("x", 4), ("y", 4))

    def on_round(number):
        if 0 < number < 5:
            reduce_end(number - 1, axes[number - 1][1])
        if number < 4:
            reduce_start(number, *axes[number])

    gather(1, row_s, col_s, second_product, on_round)

    trace_cubic, trace_quartic, spread = (
        jnp.sum(sums[4, n], keepdims=True) for n in range(3)
    )
    electrons = F32(rows * 8 // 2)
    factor = (electrons - (4.0 * trace_cubic - 3.0 * trace_quartic)) / (spread + 1e-06)
    for i in range(per):
        for j in range(3):
            three, four = cubic[block(i, j)], quartic[block(i, j)]
            value = 4.0 * three - 3.0 * four + factor * (square[block(i, j)] - 2.0 * three + four)
            moved[r * per + i, :, j * bs:(j + 1) * bs] = (value * kept(i, j)).astype(BF16)

    def moved_rows(core, away, lane_sign):
        source = lax.rem(z - lane_sign * away + 8, 4) * 2 + core
        return moved.at[pl.ds(source * per, per)]

    for away in (0, 1, 3, 2):
        piece = moved_rows(p, away, sign)
        if away:
            arrived(piece, end_sem.at[away])
        for step, direction in ((1, fwd), (3, bwd)):
            if away == 0 or (away == 1 and step == 1):
                send(piece, piece, end_sem.at[(away + step) % 4], direction["z"])
        send(piece, piece, end_sib_sem.at[away], peers["p", 1])

    slots = out.shape[0] // bs

    def place(i, state):
        count, sources = state
        mine = jnp.where(owner[i] == r, 1, 0)
        sources = tuple(
            jnp.where((mine == 1) & (count == s), i, v) for s, v in enumerate(sources)
        )
        return count + mine, sources

    count, sources = lax.fori_loop(
        0, 8 * per, place, (jnp.int32(0), (jnp.int32(0),) * slots)
    )
    for away in range(4):
        arrived(moved_rows(1 - p, away, -sign), end_sib_sem.at[away])
    for s in range(slots):
        rows_of_slot = moved[sources[s]].astype(F32)
        out[s * bs:(s + 1) * bs, :] = jnp.where(s < count, rows_of_slot, 0.0)
    for copy in started:
        copy.wait_send()


def step(density, keep_mask, owner_map):
    rows, cols = density.shape
    half, bs = rows // 2, cols // 3
    per = rows // bs
    dma = pltpu.SemaphoreType.DMA
    return pl.pallas_call(
        kernel,
        out_shape=jax.ShapeDtypeStruct(((per + 2) * bs, cols), F32),
        in_specs=[
            pl.BlockSpec(memory_space=pltpu.VMEM),
            pl.BlockSpec(memory_space=pltpu.SMEM),
            pl.BlockSpec(memory_space=pltpu.SMEM),
        ],
        out_specs=pl.BlockSpec(memory_space=pltpu.VMEM),
        scratch_shapes=[
            pltpu.VMEM((2, 16, half, cols), BF16),
            pltpu.VMEM((2, 16, half, cols), BF16),
            pltpu.VMEM((16, half, cols), BF16),
            pltpu.VMEM((16, half, cols), BF16),
            pltpu.VMEM((rows, cols), F32),
            pltpu.VMEM((rows, cols), F32),
            pltpu.VMEM((rows, cols), F32),
            pltpu.VMEM((8 * per, bs, cols), BF16),
            pltpu.VMEM((5, 3, 8, bs), F32),
            pltpu.VMEM((4, 3, 3, 8, bs), F32),
            dma((96,)),
            dma((2, 2, 16)),
            dma((2, 4)),
            dma((2, 4)),
            dma((4,)),
            dma((4,)),
            dma((4, 3)),
        ],
        compiler_params=pltpu.CompilerParams(
            collective_id=0, has_side_effects=True, vmem_limit_bytes=56 << 20
        ),
    )(density, keep_mask, owner_map)


def solution(mesh):
    return jax.shard_map(
        step,
        mesh=mesh,
        in_specs=(P("row", "col"), P(), P()),
        out_specs=P("row", "col"),
        check_vma=False,
    )
```

```python
import jax
import jax.numpy as jnp
from jax import lax
from jax.experimental import pallas as pl
from jax.experimental.pallas import tpu as pltpu
from jax.sharding import PartitionSpec as P

MESH = pl.DeviceIdType.MESH
F32 = jnp.float32
BF16 = jnp.bfloat16


def kernel(
    dens, keep, owner, out,
    row_c, row_s, col_c, col_s, square, cubic, quartic, moved, sums, sums_in,
    send_sem, row_sem, col_sem, sib_sem, end_sem, end_sib_sem, sum_sem,
):
    rows, cols = dens.shape
    group = rows // 2
    half = group // 2
    r = lax.axis_index("row")
    c = lax.axis_index("col")
    z, p = r // 2, r % 2
    y, x = c // 4, c % 4
    sign = 1 - 2 * p
    bs = cols // 3
    per = rows // bs
    per_group = per // 2

    def at(dz=0, dp=0, dy=0, dx=0):
        return (
            lax.rem(z + dz + 4, 4) * 2 + lax.rem(p + dp, 2),
            lax.rem(y + dy + 4, 4) * 4 + lax.rem(x + dx + 4, 4),
        )

    sibling = at(dp=1)
    fwd = {"x": at(dx=sign), "y": at(dy=sign), "z": at(dz=sign)}
    bwd = {"x": at(dx=-sign), "y": at(dy=-sign), "z": at(dz=-sign)}
    reduce_peers = (
        [at(dz=k // 2, dp=k % 2) for k in range(1, 8)],
        [at(dx=k) for k in range(1, 4)],
        [at(dy=k) for k in range(1, 4)],
    )

    barrier = pltpu.get_barrier_semaphore()
    for devices in reduce_peers:
        for device in devices:
            pl.semaphore_signal(barrier, inc=1, device_id=device, device_id_type=MESH)

    def block(i, j):
        return (slice(i * bs, (i + 1) * bs), slice(j * bs, (j + 1) * bs))

    def kept(i, j):
        return keep[r * per + i, c * 3 + j].astype(F32)

    for i in range(per):
        for j in range(3):
            value = (dens[block(i, j)] * kept(i, j)).astype(BF16)
            g, inner = divmod(i, per_group)
            row_c[(g, 0) + block(inner, j)] = value
            col_c[(2 * r + g,) + block(inner, j)] = value

    pl.semaphore_wait(barrier, sum(len(devices) for devices in reduce_peers))

    started = []

    def send(src, dst, recv, device):
        copy = pltpu.make_async_remote_copy(
            src_ref=src, dst_ref=dst, send_sem=send_sem.at[len(started)],
            recv_sem=recv, device_id=device, device_id_type=MESH,
        )
        copy.start()
        started.append(copy)

    def arrived(dst, recv):
        pltpu.make_async_remote_copy(
            src_ref=dst, dst_ref=dst, send_sem=send_sem.at[0],
            recv_sem=recv, device_id=sibling, device_id_type=MESH,
        ).wait_recv()

    pending = []

    def work(count):
        for _ in range(min(count, len(pending))):
            pending.pop(0)()

    order = (
        ((1, 0), (3, 0)),
        ((0, 1), (0, 3)),
        ((2, 0),),
        ((1, 1), (3, 1), (1, 3), (3, 3)),
        ((0, 2), (2, 1), (2, 3)),
        ((1, 2), (3, 2)),
        ((2, 2),),
    )
    routes = (("x", "y"), ("y", "x"))

    def slot(h, first, second):
        return 4 * second + first if h == 0 else 4 * first + second

    class Rows:
        def __init__(self, stage, g, row, ready):
            self.stage, self.g, self.row, self.ready, self.halves = stage, g, row, ready, {}

        def piece(self, h, place):
            return self.row.at[self.g, place, pl.ds(h * half, half)]

        def pass_on(self, h, first, second, which, direction):
            n = 1 if direction is fwd else 3
            there = ((first + n) % 4, second) if which == 0 else (first, (second + n) % 4)
            goal = slot(h, *there)
            send(
                self.piece(h, slot(h, first, second)), self.piece(h, goal),
                row_sem.at[self.stage, self.g, h, goal], direction[routes[h][which]],
            )

        def turn(self, h, first):
            self.pass_on(h, first, 0, 1, fwd)
            self.pass_on(h, first, 0, 1, bwd)

        def start(self):
            for h in range(2):
                self.pass_on(h, 0, 0, 0, fwd)
                self.pass_on(h, 0, 0, 0, bwd)
            for h in range(2):
                self.turn(h, 0)
            self.ready(self.g, 0)

        def round(self, number, effort=1):
            for first, second in order[number]:
                for h in range(2):
                    place = slot(h, first, second)
                    arrived(self.piece(h, place), row_sem.at[self.stage, self.g, h, place])
                    if second == 0:
                        if first == 1:
                            self.pass_on(h, 1, 0, 0, fwd)
                        self.turn(h, first)
                    elif second == 1:
                        self.pass_on(h, first, 1, 1, fwd)
                    self.halves[place] = self.halves.get(place, 0) + 1
                    if self.halves[place] == 2:
                        self.ready(self.g, place)
                    work(effort)

    class Ring:
        def __init__(self, piece, own, shared):
            self.piece, self.own, self.shared = piece, own, shared

        def at(self, core, away, lane_sign):
            return self.piece(lax.rem(z - lane_sign * away + 8, 4) * 2 + core)

        def have(self, away):
            here = self.at(p, away, sign)
            for n, direction in ((1, fwd), (3, bwd)):
                if away == 0 or (away == 1 and n == 1):
                    send(here, here, self.own.at[(away + n) % 4], direction["z"])
            send(here, here, self.shared.at[away], sibling)

        def take(self, *aways):
            for away in aways:
                arrived(self.at(p, away, sign), self.own.at[away])
                self.have(away)

        def finish(self):
            for away in range(4):
                arrived(self.at(1 - p, away, -sign), self.shared.at[away])

    def column_ring(stage, g, col):
        return Ring(lambda source: col.at[2 * source + g], col_sem.at[stage, g], sib_sem.at[stage, g])

    def move_ring(g):
        return Ring(
            lambda source: moved.at[pl.ds(source * per + g * per_group, per_group)],
            end_sem.at[g], end_sib_sem.at[g],
        )

    def column_of(place):
        behind_y, behind_x = divmod(place, 4)
        return lax.rem(y - sign * behind_y + 8, 4) * 4 + lax.rem(x - sign * behind_x + 8, 4)

    fresh = set()

    def add(name, total, g, place, row, col):
        here = pl.ds(g * group, group)
        term = jnp.dot(row[g, place], col[column_of(place)], preferred_element_type=F32)
        if (name, g) in fresh:
            total[here, :] += term
        else:
            fresh.add((name, g))
            total[here, :] = term

    waiting_c, waiting_s = [], []

    def ready_c(g, place):
        waiting_c.append(lambda: add("square", square, g, place, row_c, col_c))
        if columns_c:
            pending.append(waiting_c.pop())

    def ready_s(g, place):
        pending.append(lambda: add("cubic", cubic, g, place, row_s, col_c))
        waiting_s.append(lambda: add("quartic", quartic, g, place, row_s, col_s))
        if columns_s:
            pending.append(waiting_s.pop())

    columns_c, columns_s = [], []

    def fold(v):
        return jnp.sum(v.reshape(bs // 8, 8, bs), axis=0)

    totals = [jnp.zeros((8, bs), F32)] * 3

    def make_square(g):
        work(len(pending))
        for i in range(g * per_group, (g + 1) * per_group):
            for j in range(3):
                value = square[block(i, j)] * kept(i, j)
                square[block(i, j)] = value
                rounded = value.astype(BF16)
                inner = i - g * per_group
                row_s[(g, 0) + block(inner, j)] = rounded
                col_s[(2 * r + g,) + block(inner, j)] = rounded

    def add_sums(g):
        for i in range(g * per_group, (g + 1) * per_group):
            for j in range(3):
                inner = i - g * per_group
                value = square[block(i, j)]
                difference = dens[block(i, j)] * kept(i, j) - value
                wide = row_s[(g, 0) + block(inner, j)].astype(F32)
                one = row_c[(g, 0) + block(inner, j)].astype(F32)
                terms = (wide * one, wide * wide, difference * difference)
                for n, v in enumerate(terms):
                    totals[n] = totals[n] + fold(v)

    def reduce_start(n):
        for k, device in enumerate(reduce_peers[n]):
            send(sums.at[n], sums_in.at[n, k], sum_sem.at[n, k], device)

    def reduce_end(n):
        total = sums[n]
        for k in range(len(reduce_peers[n])):
            arrived(sums_in.at[n, k], sum_sem.at[n, k])
            total += sums_in[n, k]
        sums[n + 1] = total

    def make_result(g):
        work(len(pending))
        trace_cubic, trace_quartic, spread = (
            jnp.sum(sums[3, n], keepdims=True) for n in range(3)
        )
        electrons = F32(rows * 8 // 2)
        factor = (electrons - (4.0 * trace_cubic - 3.0 * trace_quartic)) / (spread + 1e-06)
        for i in range(g * per_group, (g + 1) * per_group):
            for j in range(3):
                three, four = cubic[block(i, j)], quartic[block(i, j)]
                value = 4.0 * three - 3.0 * four + factor * (square[block(i, j)] - 2.0 * three + four)
                moved[r * per + i, :, j * bs:(j + 1) * bs] = (value * kept(i, j)).astype(BF16)

    c0, c1 = (Rows(0, g, row_c, ready_c) for g in range(2))
    s0, s1 = (Rows(1, g, row_s, ready_s) for g in range(2))
    zc0, zc1 = (column_ring(0, g, col_c) for g in range(2))
    zs0, zs1 = (column_ring(1, g, col_s) for g in range(2))
    m0, m1 = (move_ring(g) for g in range(2))

    c0.start()
    zc0.have(0)
    zc1.have(0)
    c0.round(0)
    zc0.take(1, 3)
    c0.round(1)
    zc1.take(1, 3)
    c0.round(2)
    zc0.take(2)
    c1.start()
    c0.round(3)
    zc1.take(2)
    zc0.finish()
    zc1.finish()
    columns_c.append(True)
    pending += waiting_c
    waiting_c.clear()
    c0.round(4, 2)
    c1.round(0, 2)
    c0.round(5, 2)
    c1.round(1, 2)
    c0.round(6, 2)
    make_square(0)
    zs0.have(0)
    c1.round(2)
    s0.start()
    c1.round(3)
    add_sums(0)
    c1.round(4)
    zs0.take(1, 3)
    s0.round(0)
    c1.round(5)
    c1.round(6)
    make_square(1)
    zs1.have(0)
    add_sums(1)
    for n in range(3):
        sums[0, n] = totals[n]
    reduce_start(0)
    zs0.take(2)
    s0.round(1)
    reduce_end(0)
    reduce_start(1)
    s0.round(2)
    zs1.take(1, 3)
    s1.start()
    reduce_end(1)
    reduce_start(2)
    s0.round(3)
    zs1.take(2)
    zs0.finish()
    zs1.finish()
    columns_s.append(True)
    pending += waiting_s
    waiting_s.clear()
    s0.round(4, 3)
    reduce_end(2)
    s1.round(0, 3)
    s0.round(5, 3)
    s1.round(1, 3)
    s0.round(6, 3)
    make_result(0)
    m0.have(0)
    s1.round(2, 2)
    s1.round(3, 2)
    m0.take(1, 3)
    s1.round(4, 2)
    s1.round(5, 2)
    m0.take(2)
    s1.round(6, 2)
    make_result(1)
    m1.have(0)

    slots = out.shape[0] // bs

    def place(i, state):
        count, sources = state
        mine = jnp.where(owner[i] == r, 1, 0)
        sources = tuple(
            jnp.where((mine == 1) & (count == s), i, v) for s, v in enumerate(sources)
        )
        return count + mine, sources

    count, sources = lax.fori_loop(
        0, 8 * per, place, (jnp.int32(0), (jnp.int32(0),) * slots)
    )
    m1.take(1, 3, 2)
    m0.finish()
    m1.finish()
    for s in range(slots):
        found = moved[sources[s]]
        out[s * bs:(s + 1) * bs, :] = jnp.where(s < count, found, jnp.zeros_like(found))
    for copy in started:
        copy.wait_send()


def step(density, keep_mask, owner_map):
    rows, cols = density.shape
    group, bs = rows // 2, cols // 3
    per = rows // bs
    dma = pltpu.SemaphoreType.DMA
    return pl.pallas_call(
        kernel,
        out_shape=jax.ShapeDtypeStruct(((per + 2) * bs, cols), BF16),
        in_specs=[
            pl.BlockSpec(memory_space=pltpu.VMEM),
            pl.BlockSpec(memory_space=pltpu.SMEM),
            pl.BlockSpec(memory_space=pltpu.SMEM),
        ],
        out_specs=pl.BlockSpec(memory_space=pltpu.VMEM),
        scratch_shapes=[
            pltpu.VMEM((2, 16, group, cols), BF16),
            pltpu.VMEM((2, 16, group, cols), BF16),
            pltpu.VMEM((16, group, cols), BF16),
            pltpu.VMEM((16, group, cols), BF16),
            pltpu.VMEM((rows, cols), F32),
            pltpu.VMEM((rows, cols), F32),
            pltpu.VMEM((rows, cols), F32),
            pltpu.VMEM((8 * per, bs, cols), BF16),
            pltpu.VMEM((4, 3, 8, bs), F32),
            pltpu.VMEM((3, 7, 3, 8, bs), F32),
            dma((180,)),
            dma((2, 2, 2, 16)),
            dma((2, 2, 4)),
            dma((2, 2, 4)),
            dma((2, 4)),
            dma((2, 4)),
            dma((3, 7)),
        ],
        compiler_params=pltpu.CompilerParams(
            collective_id=0, has_side_effects=True, vmem_limit_bytes=56 << 20
        ),
    )(density, keep_mask, owner_map).astype(F32)


def solution(mesh):
    return jax.shard_map(
        step,
        mesh=mesh,
        in_specs=(P("row", "col"), P(), P()),
        out_specs=P("row", "col"),
        check_vma=False,
    )
```

```python
import jax
import jax.numpy as jnp
from jax import lax
from jax.experimental import pallas as pl
from jax.experimental.pallas import tpu as pltpu
from jax.sharding import PartitionSpec as P

MESH = pl.DeviceIdType.MESH
F32 = jnp.float32
BF16 = jnp.bfloat16


def dense_kernel(
    dens, keep, owner, out,
    row_c, row_s, col_c, col_s, square, cubic, quartic, moved, sums, sums_in,
    send_sem, row_sem, col_sem, sib_sem, end_sem, end_sib_sem, sum_sem,
):
    rows, cols = dens.shape
    group = rows // 2
    half = group // 2
    r = lax.axis_index("row")
    c = lax.axis_index("col")
    z, p = r // 2, r % 2
    y, x = c // 4, c % 4
    sign = 1 - 2 * p
    bs = cols // 3
    per = rows // bs
    per_group = per // 2

    def at(dz=0, dp=0, dy=0, dx=0):
        return (
            lax.rem(z + dz + 4, 4) * 2 + lax.rem(p + dp, 2),
            lax.rem(y + dy + 4, 4) * 4 + lax.rem(x + dx + 4, 4),
        )

    sibling = at(dp=1)
    fwd = {"x": at(dx=sign), "y": at(dy=sign), "z": at(dz=sign)}
    bwd = {"x": at(dx=-sign), "y": at(dy=-sign), "z": at(dz=-sign)}
    reduce_peers = (
        [at(dz=k // 2, dp=k % 2) for k in range(1, 8)],
        [at(dx=k) for k in range(1, 4)],
        [at(dy=k) for k in range(1, 4)],
    )

    barrier = pltpu.get_barrier_semaphore()
    for devices in reduce_peers:
        for device in devices:
            pl.semaphore_signal(barrier, inc=1, device_id=device, device_id_type=MESH)

    def block(i, j):
        return (slice(i * bs, (i + 1) * bs), slice(j * bs, (j + 1) * bs))

    def kept(i, j):
        return keep[r * per + i, c * 3 + j].astype(F32)

    for i in range(per):
        for j in range(3):
            value = (dens[block(i, j)] * kept(i, j)).astype(BF16)
            g, inner = divmod(i, per_group)
            row_c[(g, 0) + block(inner, j)] = value
            col_c[(2 * r + g,) + block(inner, j)] = value

    pl.semaphore_wait(barrier, sum(len(devices) for devices in reduce_peers))

    started = []

    def send(src, dst, recv, device):
        copy = pltpu.make_async_remote_copy(
            src_ref=src, dst_ref=dst, send_sem=send_sem.at[len(started)],
            recv_sem=recv, device_id=device, device_id_type=MESH,
        )
        copy.start()
        started.append(copy)

    def arrived(dst, recv):
        pltpu.make_async_remote_copy(
            src_ref=dst, dst_ref=dst, send_sem=send_sem.at[0],
            recv_sem=recv, device_id=sibling, device_id_type=MESH,
        ).wait_recv()

    order = (
        ((1, 0), (3, 0)),
        ((0, 1), (0, 3)),
        ((2, 0),),
        ((1, 1), (3, 1), (1, 3), (3, 3)),
        ((0, 2), (2, 1), (2, 3)),
        ((1, 2), (3, 2)),
        ((2, 2),),
    )
    routes = (("x", "y"), ("y", "x"))

    def slot(h, first, second):
        return 4 * second + first if h == 0 else 4 * first + second

    class Rows:
        def __init__(self, stage, g, row):
            self.stage, self.g, self.row = stage, g, row

        def piece(self, h, place):
            return self.row.at[self.g, place, pl.ds(h * half, half)]

        def pass_on(self, h, first, second, which, direction):
            n = 1 if direction is fwd else 3
            there = ((first + n) % 4, second) if which == 0 else (first, (second + n) % 4)
            goal = slot(h, *there)
            send(
                self.piece(h, slot(h, first, second)), self.piece(h, goal),
                row_sem.at[self.stage, self.g, h, goal], direction[routes[h][which]],
            )

        def turn(self, h, first):
            self.pass_on(h, first, 0, 1, fwd)
            self.pass_on(h, first, 0, 1, bwd)

        def start(self):
            for h in range(2):
                self.pass_on(h, 0, 0, 0, fwd)
                self.pass_on(h, 0, 0, 0, bwd)
            for h in range(2):
                self.turn(h, 0)

        def round(self, number):
            for first, second in order[number]:
                for h in range(2):
                    place = slot(h, first, second)
                    arrived(self.piece(h, place), row_sem.at[self.stage, self.g, h, place])
                    if second == 0:
                        if first == 1:
                            self.pass_on(h, 1, 0, 0, fwd)
                        self.turn(h, first)
                    elif second == 1:
                        self.pass_on(h, first, 1, 1, fwd)

    class Ring:
        def __init__(self, piece, own, shared):
            self.piece, self.own, self.shared = piece, own, shared

        def at(self, core, away, lane_sign):
            return self.piece(lax.rem(z - lane_sign * away + 8, 4) * 2 + core)

        def have(self, away):
            here = self.at(p, away, sign)
            for n, direction in ((1, fwd), (3, bwd)):
                if away == 0 or (away == 1 and n == 1):
                    send(here, here, self.own.at[(away + n) % 4], direction["z"])
            send(here, here, self.shared.at[away], sibling)

        def take(self, *aways):
            for away in aways:
                arrived(self.at(p, away, sign), self.own.at[away])
                self.have(away)

        def finish(self):
            for away in range(4):
                arrived(self.at(1 - p, away, -sign), self.shared.at[away])

    def column_ring(stage, g, col):
        return Ring(lambda source: col.at[2 * source + g], col_sem.at[stage, g], sib_sem.at[stage, g])

    def move_ring(g):
        return Ring(
            lambda source: moved.at[pl.ds(source * per + g * per_group, per_group)],
            end_sem.at[g], end_sib_sem.at[g],
        )

    def multiply(g, row, *pairs):
        here = pl.ds(g * group, group)
        for total, _ in pairs:
            total[here, :] = jnp.zeros((group, cols), F32)

        def one(place, carry):
            behind_y, behind_x = place // 4, place % 4
            k = lax.rem(y - sign * behind_y + 8, 4) * 4 + lax.rem(x - sign * behind_x + 8, 4)
            for total, col in pairs:
                total[here, :] += jnp.dot(row[g, place], col[k], preferred_element_type=F32)
            return carry

        lax.fori_loop(0, 16, one, 0)

    def fold(v):
        return jnp.sum(v.reshape(bs // 8, 8, bs), axis=0)

    totals = [jnp.zeros((8, bs), F32)] * 3

    def make_square(g):
        multiply(g, row_c, (square, col_c))
        for i in range(g * per_group, (g + 1) * per_group):
            for j in range(3):
                value = square[block(i, j)] * kept(i, j)
                square[block(i, j)] = value
                rounded = value.astype(BF16)
                inner = i - g * per_group
                row_s[(g, 0) + block(inner, j)] = rounded
                col_s[(2 * r + g,) + block(inner, j)] = rounded

    def add_sums(g):
        for i in range(g * per_group, (g + 1) * per_group):
            for j in range(3):
                inner = i - g * per_group
                value = square[block(i, j)]
                difference = dens[block(i, j)] * kept(i, j) - value
                wide = row_s[(g, 0) + block(inner, j)].astype(F32)
                one = row_c[(g, 0) + block(inner, j)].astype(F32)
                terms = (wide * one, wide * wide, difference * difference)
                for n, v in enumerate(terms):
                    totals[n] = totals[n] + fold(v)

    def reduce_start(n):
        for k, device in enumerate(reduce_peers[n]):
            send(sums.at[n], sums_in.at[n, k], sum_sem.at[n, k], device)

    def reduce_end(n):
        total = sums[n]
        for k in range(len(reduce_peers[n])):
            arrived(sums_in.at[n, k], sum_sem.at[n, k])
            total += sums_in[n, k]
        sums[n + 1] = total

    def make_result(g):
        multiply(g, row_s, (cubic, col_c), (quartic, col_s))
        trace_cubic, trace_quartic, spread = (
            jnp.sum(sums[3, n], keepdims=True) for n in range(3)
        )
        electrons = F32(rows * 8 // 2)
        factor = (electrons - (4.0 * trace_cubic - 3.0 * trace_quartic)) / (spread + 1e-06)
        for i in range(g * per_group, (g + 1) * per_group):
            for j in range(3):
                three, four = cubic[block(i, j)], quartic[block(i, j)]
                value = 4.0 * three - 3.0 * four + factor * (square[block(i, j)] - 2.0 * three + four)
                moved[r * per + i, :, j * bs:(j + 1) * bs] = (value * kept(i, j)).astype(BF16)

    c0, c1 = (Rows(0, g, row_c) for g in range(2))
    s0, s1 = (Rows(1, g, row_s) for g in range(2))
    zc0, zc1 = (column_ring(0, g, col_c) for g in range(2))
    zs0, zs1 = (column_ring(1, g, col_s) for g in range(2))
    m0, m1 = (move_ring(g) for g in range(2))

    c0.start()
    zc0.have(0)
    zc1.have(0)
    c0.round(0)
    zc0.take(1, 3)
    c0.round(1)
    zc1.take(1, 3)
    c0.round(2)
    zc0.take(2)
    c1.start()
    c0.round(3)
    zc1.take(2)
    zc0.finish()
    zc1.finish()
    c0.round(4)
    c1.round(0)
    c0.round(5)
    c1.round(1)
    c0.round(6)
    make_square(0)
    zs0.have(0)
    c1.round(2)
    s0.start()
    c1.round(3)
    add_sums(0)
    c1.round(4)
    zs0.take(1, 3)
    s0.round(0)
    c1.round(5)
    c1.round(6)
    make_square(1)
    zs1.have(0)
    add_sums(1)
    for n in range(3):
        sums[0, n] = totals[n]
    reduce_start(0)
    zs0.take(2)
    s0.round(1)
    reduce_end(0)
    reduce_start(1)
    s0.round(2)
    zs1.take(1, 3)
    s1.start()
    reduce_end(1)
    reduce_start(2)
    s0.round(3)
    zs1.take(2)
    zs0.finish()
    zs1.finish()
    s0.round(4)
    reduce_end(2)
    s1.round(0)
    s0.round(5)
    s1.round(1)
    s0.round(6)
    make_result(0)
    m0.have(0)
    s1.round(2)
    s1.round(3)
    m0.take(1, 3)
    s1.round(4)
    s1.round(5)
    m0.take(2)
    s1.round(6)
    make_result(1)
    m1.have(0)

    slots = out.shape[0] // bs

    def place(i, state):
        count, sources = state
        mine = jnp.where(owner[i] == r, 1, 0)
        sources = tuple(
            jnp.where((mine == 1) & (count == s), i, v) for s, v in enumerate(sources)
        )
        return count + mine, sources

    count, sources = lax.fori_loop(
        0, 8 * per, place, (jnp.int32(0), (jnp.int32(0),) * slots)
    )
    m1.take(1, 3, 2)
    m0.finish()
    m1.finish()
    for s in range(slots):
        found = moved[sources[s]]
        out[s * bs:(s + 1) * bs, :] = jnp.where(s < count, found, jnp.zeros_like(found))
    for copy in started:
        copy.wait_send()


def dense_step(density, keep_mask, owner_map):
    rows, cols = density.shape
    group, bs = rows // 2, cols // 3
    per = rows // bs
    dma = pltpu.SemaphoreType.DMA
    return pl.pallas_call(
        dense_kernel,
        out_shape=jax.ShapeDtypeStruct(((per + 2) * bs, cols), BF16),
        in_specs=[
            pl.BlockSpec(memory_space=pltpu.VMEM),
            pl.BlockSpec(memory_space=pltpu.SMEM),
            pl.BlockSpec(memory_space=pltpu.SMEM),
        ],
        out_specs=pl.BlockSpec(memory_space=pltpu.VMEM),
        scratch_shapes=[
            pltpu.VMEM((2, 16, group, cols), BF16),
            pltpu.VMEM((2, 16, group, cols), BF16),
            pltpu.VMEM((16, group, cols), BF16),
            pltpu.VMEM((16, group, cols), BF16),
            pltpu.VMEM((rows, cols), F32),
            pltpu.VMEM((rows, cols), F32),
            pltpu.VMEM((rows, cols), F32),
            pltpu.VMEM((8 * per, bs, cols), BF16),
            pltpu.VMEM((4, 3, 8, bs), F32),
            pltpu.VMEM((3, 7, 3, 8, bs), F32),
            dma((180,)),
            dma((2, 2, 2, 16)),
            dma((2, 2, 4)),
            dma((2, 2, 4)),
            dma((2, 4)),
            dma((2, 4)),
            dma((3, 7)),
        ],
        compiler_params=pltpu.CompilerParams(
            collective_id=1, has_side_effects=True, vmem_limit_bytes=56 << 20
        ),
    )(density, keep_mask, owner_map)


LIST = 12


def packed_kernel(
    dens, keep, owner, out,
    blocks, col_c, col_s, left, square, cubic, quartic, moved, sums, sums_in, spots, spots_here,
    send_sem, row_sem, col_sem, sib_sem, end_sem, end_sib_sem, sum_sem, *lists,
):
    rows, cols = dens.shape
    bs = cols // 3
    per = rows // bs
    tile = per * 3
    list_c, list_s = lists[:16], lists[16:]
    half = LIST // 2
    r = lax.axis_index("row")
    c = lax.axis_index("col")
    z, p = r // 2, r % 2
    y, x = c // 4, c % 4
    sign = 1 - 2 * p

    def at(dz=0, dp=0, dy=0, dx=0):
        return (
            lax.rem(z + dz + 4, 4) * 2 + lax.rem(p + dp, 2),
            lax.rem(y + dy + 4, 4) * 4 + lax.rem(x + dx + 4, 4),
        )

    sibling = at(dp=1)
    fwd = {"x": at(dx=sign), "y": at(dy=sign), "z": at(dz=sign)}
    bwd = {"x": at(dx=-sign), "y": at(dy=-sign), "z": at(dz=-sign)}
    reduce_peers = (
        [at(dz=k // 2, dp=k % 2) for k in range(1, 8)],
        [at(dy=k // 4, dx=k % 4) for k in range(1, 16)],
    )

    barrier = pltpu.get_barrier_semaphore()
    for devices in reduce_peers:
        for device in devices:
            pl.semaphore_signal(barrier, inc=1, device_id=device, device_id_type=MESH)

    def block(i, j):
        return (slice(i * bs, (i + 1) * bs), slice(j * bs, (j + 1) * bs))

    def kept(i, j):
        return keep[r * per + i, c * 3 + j].astype(F32)

    def col_block(i, j):
        return (2 * r + i // (per // 2),) + block(i % (per // 2), j)

    for i in range(per):
        for j in range(3):
            value = (dens[block(i, j)] * kept(i, j)).astype(BF16)
            blocks[i * 3 + j] = value
            col_c[col_block(i, j)] = value

    def find(b, state):
        count, sources = state
        one = keep[r * per + b // 3, c * 3 + b % 3]
        sources = tuple(
            jnp.where((one == 1) & (count == s), b, v) for s, v in enumerate(sources)
        )
        return count + one, sources

    _, listed = lax.fori_loop(0, tile, find, (jnp.int32(0), (jnp.int32(0),) * LIST))

    def pack(target):
        for s in range(LIST):
            target[s] = blocks[listed[s]]

    pack(list_c[0])
    pl.semaphore_wait(barrier, sum(len(devices) for devices in reduce_peers))

    started = []

    def send(src, dst, recv, device):
        copy = pltpu.make_async_remote_copy(
            src_ref=src, dst_ref=dst, send_sem=send_sem.at[len(started)],
            recv_sem=recv, device_id=device, device_id_type=MESH,
        )
        copy.start()
        started.append(copy)

    def arrived(dst, recv):
        pltpu.make_async_remote_copy(
            src_ref=dst, dst_ref=dst, send_sem=send_sem.at[0],
            recv_sem=recv, device_id=sibling, device_id_type=MESH,
        ).wait_recv()

    pending = []

    def work(count):
        for _ in range(min(count, len(pending))):
            pending.pop(0)()

    routes = (("x", "y"), ("y", "x"))

    def slot(h, first, second):
        return 4 * second + first if h == 0 else 4 * first + second

    class Rows:
        def __init__(self, stage, row, ready):
            self.stage, self.row, self.ready, self.halves = stage, row, ready, {}

        def piece(self, h, place):
            return self.row[place].at[pl.ds(h * half, half)]

        def pass_on(self, h, first, second, which, direction):
            n = 1 if direction is fwd else 3
            there = ((first + n) % 4, second) if which == 0 else (first, (second + n) % 4)
            goal = slot(h, *there)
            send(
                self.piece(h, slot(h, first, second)), self.piece(h, goal),
                row_sem.at[self.stage, h, goal], direction[routes[h][which]],
            )

        def turn(self, h, first):
            self.pass_on(h, first, 0, 1, fwd)
            self.pass_on(h, first, 0, 1, bwd)

        def start(self):
            for h in range(2):
                self.pass_on(h, 0, 0, 0, fwd)
                self.pass_on(h, 0, 0, 0, bwd)
            for h in range(2):
                self.turn(h, 0)
            self.ready(0)

        def take(self, *pieces, effort=1):
            for first, second in pieces:
                for h in range(2):
                    place = slot(h, first, second)
                    arrived(self.piece(h, place), row_sem.at[self.stage, h, place])
                    if second == 0:
                        if first == 1:
                            self.pass_on(h, 1, 0, 0, fwd)
                        self.turn(h, first)
                    elif second == 1:
                        self.pass_on(h, first, 1, 1, fwd)
                    self.halves[place] = self.halves.get(place, 0) + 1
                    if self.halves[place] == 2:
                        self.ready(place)
                    work(effort)

    class Ring:
        def __init__(self, piece, own, shared):
            self.piece, self.own, self.shared = piece, own, shared

        def at(self, core, away, lane_sign):
            return self.piece(lax.rem(z - lane_sign * away + 8, 4) * 2 + core)

        def have(self, away):
            here = self.at(p, away, sign)
            for n, direction in ((1, fwd), (3, bwd)):
                if away == 0 or (away == 1 and n == 1):
                    send(here, here, self.own.at[(away + n) % 4], direction["z"])
            send(here, here, self.shared.at[away], sibling)

        def take(self, *aways):
            for away in aways:
                arrived(self.at(p, away, sign), self.own.at[away])
                self.have(away)

        def finish(self):
            for away in range(4):
                arrived(self.at(1 - p, away, -sign), self.shared.at[away])

    def columns(stage, col):
        return Ring(lambda source: col.at[pl.ds(2 * source, 2)], col_sem.at[stage], sib_sem.at[stage])

    def column_of(place):
        behind_y, behind_x = divmod(place, 4)
        return lax.rem(y - sign * behind_y + 8, 4) * 4 + lax.rem(x - sign * behind_x + 8, 4)

    def spread(row, place):
        source = column_of(place)
        for i in range(per):
            for j in range(3):
                found = row[place][spots[source * tile + i * 3 + j]]
                there = keep[r * per + i, source * 3 + j] == 1
                left[block(i, j)] = jnp.where(there, found, jnp.zeros_like(found))

    fresh = set()

    def add(name, total, place, col):
        term = jnp.dot(left[...], col[column_of(place)], preferred_element_type=F32)
        if name in fresh:
            total[...] += term
        else:
            fresh.add(name)
            total[...] = term

    waiting = []
    columns_ready = []

    def first_product(place):
        spread(list_c, place)
        add("square", square, place, col_c)

    def second_product(place):
        spread(list_s, place)
        add("cubic", cubic, place, col_c)
        add("quartic", quartic, place, col_s)

    def ready_for(product):
        def ready(place):
            waiting.append(lambda: product(place))
            if columns_ready:
                pending.append(waiting.pop())
        return ready

    def now_columns():
        columns_ready.append(True)
        pending.extend(waiting)
        waiting.clear()

    rows_c = Rows(0, list_c, ready_for(first_product))
    rows_s = Rows(1, list_s, ready_for(second_product))
    ring_c, ring_s = columns(0, col_c), columns(1, col_s)

    rows_c.start()
    ring_c.have(0)

    def number(t, count):
        count = jnp.where(t % tile == 0, 0, count)
        spots[t] = jnp.minimum(count, LIST - 1)
        return count + keep[r * per + t % tile // 3, t // tile * 3 + t % 3]

    lax.fori_loop(0, 16 * tile, number, jnp.int32(0))

    rows_c.take((1, 0), (3, 0))
    ring_c.take(1, 3)
    rows_c.take((0, 1), (0, 3))
    rows_c.take((2, 0))
    ring_c.take(2)
    rows_c.take((1, 1), (3, 1), (1, 3), (3, 3))
    ring_c.finish()
    now_columns()
    rows_c.take((0, 2), (2, 1), (2, 3), effort=2)
    rows_c.take((1, 2), (3, 2), effort=2)
    rows_c.take((2, 2), effort=2)
    work(len(pending))
    columns_ready.clear()

    for i in range(per):
        for j in range(3):
            value = square[block(i, j)] * kept(i, j)
            square[block(i, j)] = value
            rounded = value.astype(BF16)
            col_s[col_block(i, j)] = rounded
            blocks[i * 3 + j] = rounded
    pack(list_s[0])
    rows_s.start()
    ring_s.have(0)

    def fold(v):
        return jnp.sum(v.reshape(bs // 8, 8, bs), axis=0)

    totals = [jnp.zeros((8, bs), F32)] * 3
    for i in range(per):
        for j in range(3):
            value = square[block(i, j)]
            difference = dens[block(i, j)] * kept(i, j) - value
            wide = blocks[i * 3 + j].astype(F32)
            one = col_c[col_block(i, j)].astype(F32)
            terms = (wide * one, wide * wide, difference * difference)
            totals = [t + fold(v) for t, v in zip(totals, terms, strict=True)]
    sums[0] = jnp.zeros((8, bs), F32)
    for n in range(3):
        sums[0, n:n + 1] = jnp.sum(totals[n], axis=0, keepdims=True)

    def reduce_start(n):
        for k, device in enumerate(reduce_peers[n]):
            send(sums.at[n], sums_in.at[n, k], sum_sem.at[n, k], device)

    def reduce_end(n):
        total = sums[n]
        for k in range(len(reduce_peers[n])):
            arrived(sums_in.at[n, k], sum_sem.at[n, k])
            total += sums_in[n, k]
        sums[n + 1] = total

    reduce_start(0)
    rows_s.take((1, 0), (3, 0))
    ring_s.take(1, 3)
    rows_s.take((0, 1), (0, 3))
    rows_s.take((2, 0))
    ring_s.take(2)
    rows_s.take((1, 1), (3, 1), (1, 3), (3, 3))
    reduce_end(0)
    reduce_start(1)
    ring_s.finish()
    now_columns()
    rows_s.take((0, 2), (2, 1), (2, 3), effort=2)
    rows_s.take((1, 2), (3, 2), effort=2)
    rows_s.take((2, 2), effort=2)
    work(len(pending))
    reduce_end(1)

    trace_cubic, trace_quartic, spread_sum = (
        jnp.sum(sums[2, n:n + 1], keepdims=True) for n in range(3)
    )
    electrons = F32(rows * 8 // 2)
    factor = (electrons - (4.0 * trace_cubic - 3.0 * trace_quartic)) / (spread_sum + 1e-06)
    for i in range(per):
        for j in range(3):
            three, four = cubic[block(i, j)], quartic[block(i, j)]
            value = 4.0 * three - 3.0 * four + factor * (square[block(i, j)] - 2.0 * three + four)
            blocks[i * 3 + j] = (value * kept(i, j)).astype(BF16)
    for s in range(LIST):
        moved[r * LIST + s] = blocks[listed[s]]
    ring_t = Ring(lambda source: moved.at[pl.ds(source * LIST, LIST)], end_sem, end_sib_sem)
    ring_t.have(0)

    slots = out.shape[0] // bs

    def number_here(t, count):
        count = jnp.where(t % tile == 0, 0, count)
        spots_here[t] = jnp.minimum(count, LIST - 1) + t // tile * LIST
        return count + keep[t // 3, c * 3 + t % 3]

    lax.fori_loop(0, 8 * tile, number_here, jnp.int32(0))

    def place_rows(i, state):
        count, sources = state
        one = jnp.where(owner[i] == r, 1, 0)
        sources = tuple(
            jnp.where((one == 1) & (count == s), i, v) for s, v in enumerate(sources)
        )
        return count + one, sources

    count, sources = lax.fori_loop(
        0, 8 * per, place_rows, (jnp.int32(0), (jnp.int32(0),) * slots)
    )
    ring_t.take(1, 3, 2)
    ring_t.finish()
    for s in range(slots):
        for j in range(3):
            found = moved[spots_here[sources[s] * 3 + j]]
            there = (s < count) & (keep[sources[s], c * 3 + j] == 1)
            out[block(s, j)] = jnp.where(there, found, jnp.zeros_like(found))
    for copy in started:
        copy.wait_send()


def packed_step(density, keep_mask, owner_map):
    rows, cols = density.shape
    bs = cols // 3
    per = rows // bs
    dma = pltpu.SemaphoreType.DMA
    return pl.pallas_call(
        packed_kernel,
        out_shape=jax.ShapeDtypeStruct(((per + 2) * bs, cols), BF16),
        in_specs=[
            pl.BlockSpec(memory_space=pltpu.VMEM),
            pl.BlockSpec(memory_space=pltpu.SMEM),
            pl.BlockSpec(memory_space=pltpu.SMEM),
        ],
        out_specs=pl.BlockSpec(memory_space=pltpu.VMEM),
        scratch_shapes=[
            pltpu.VMEM((per * 3, bs, bs), BF16),
            pltpu.VMEM((16, cols, cols), BF16),
            pltpu.VMEM((16, cols, cols), BF16),
            pltpu.VMEM((rows, cols), BF16),
            pltpu.VMEM((rows, cols), F32),
            pltpu.VMEM((rows, cols), F32),
            pltpu.VMEM((rows, cols), F32),
            pltpu.VMEM((8 * LIST, bs, bs), BF16),
            pltpu.VMEM((3, 8, bs), F32),
            pltpu.VMEM((2, 15, 8, bs), F32),
            pltpu.SMEM((16 * per * 3,), jnp.int32),
            pltpu.SMEM((8 * per * 3,), jnp.int32),
            dma((108,)),
            dma((2, 2, 16)),
            dma((2, 4)),
            dma((2, 4)),
            dma((4,)),
            dma((4,)),
            dma((2, 15)),
        ] + [pltpu.VMEM((LIST, bs, bs), BF16)] * 32,
        compiler_params=pltpu.CompilerParams(
            collective_id=0, has_side_effects=True, vmem_limit_bytes=56 << 20
        ),
    )(density, keep_mask, owner_map)


def step(density, keep_mask, owner_map):
    rows = lax.axis_size("row")
    cols = lax.axis_size("col")
    blocks = keep_mask.shape[0]
    kept = keep_mask.reshape(rows, blocks // rows, cols, blocks // cols).sum(axis=(1, 3))
    return lax.cond(
        jnp.max(kept) <= LIST, packed_step, dense_step, density, keep_mask, owner_map
    ).astype(F32)


def solution(mesh):
    return jax.shard_map(
        step,
        mesh=mesh,
        in_specs=(P("row", "col"), P(), P()),
        out_specs=P("row", "col"),
        check_vma=False,
    )
```

```python
import jax
import jax.numpy as jnp
from jax import lax
from jax.experimental import pallas as pl
from jax.experimental.pallas import tpu as pltpu
from jax.sharding import PartitionSpec as P

MESH = pl.DeviceIdType.MESH
F32 = jnp.float32
BF16 = jnp.bfloat16


def dense_kernel(
    dens, keep, owner, out,
    row_c, row_s, col_c, col_s, square, cubic, quartic, moved, sums, sums_in,
    send_sem, row_sem, col_sem, sib_sem, end_sem, end_sib_sem, sum_sem,
):
    rows, cols = dens.shape
    group = rows // 2
    half = group // 2
    r = lax.axis_index("row")
    c = lax.axis_index("col")
    z, p = r // 2, r % 2
    y, x = c // 4, c % 4
    sign = 1 - 2 * p
    bs = cols // 3
    per = rows // bs
    per_group = per // 2

    def at(dz=0, dp=0, dy=0, dx=0):
        return (
            lax.rem(z + dz + 4, 4) * 2 + lax.rem(p + dp, 2),
            lax.rem(y + dy + 4, 4) * 4 + lax.rem(x + dx + 4, 4),
        )

    sibling = at(dp=1)
    fwd = {"x": at(dx=sign), "y": at(dy=sign), "z": at(dz=sign)}
    bwd = {"x": at(dx=-sign), "y": at(dy=-sign), "z": at(dz=-sign)}
    reduce_peers = (
        [at(dz=k // 2, dp=k % 2) for k in range(1, 8)],
        [at(dx=k) for k in range(1, 4)],
        [at(dy=k) for k in range(1, 4)],
    )

    barrier = pltpu.get_barrier_semaphore()
    for devices in reduce_peers:
        for device in devices:
            pl.semaphore_signal(barrier, inc=1, device_id=device, device_id_type=MESH)

    def block(i, j):
        return (slice(i * bs, (i + 1) * bs), slice(j * bs, (j + 1) * bs))

    def kept(i, j):
        return keep[r * per + i, c * 3 + j].astype(F32)

    for i in range(per):
        for j in range(3):
            value = (dens[block(i, j)] * kept(i, j)).astype(BF16)
            g, inner = divmod(i, per_group)
            row_c[(g, 0) + block(inner, j)] = value
            col_c[(2 * r + g,) + block(inner, j)] = value

    pl.semaphore_wait(barrier, sum(len(devices) for devices in reduce_peers))

    started = []

    def send(src, dst, recv, device):
        copy = pltpu.make_async_remote_copy(
            src_ref=src, dst_ref=dst, send_sem=send_sem.at[len(started)],
            recv_sem=recv, device_id=device, device_id_type=MESH,
        )
        copy.start()
        started.append(copy)

    def arrived(dst, recv):
        pltpu.make_async_remote_copy(
            src_ref=dst, dst_ref=dst, send_sem=send_sem.at[0],
            recv_sem=recv, device_id=sibling, device_id_type=MESH,
        ).wait_recv()

    order = (
        ((1, 0), (3, 0)),
        ((0, 1), (0, 3)),
        ((2, 0),),
        ((1, 1), (3, 1), (1, 3), (3, 3)),
        ((0, 2), (2, 1), (2, 3)),
        ((1, 2), (3, 2)),
        ((2, 2),),
    )
    routes = (("x", "y"), ("y", "x"))

    def slot(h, first, second):
        return 4 * second + first if h == 0 else 4 * first + second

    class Rows:
        def __init__(self, stage, g, row):
            self.stage, self.g, self.row = stage, g, row

        def piece(self, h, place):
            return self.row.at[self.g, place, pl.ds(h * half, half)]

        def pass_on(self, h, first, second, which, direction):
            n = 1 if direction is fwd else 3
            there = ((first + n) % 4, second) if which == 0 else (first, (second + n) % 4)
            goal = slot(h, *there)
            send(
                self.piece(h, slot(h, first, second)), self.piece(h, goal),
                row_sem.at[self.stage, self.g, h, goal], direction[routes[h][which]],
            )

        def turn(self, h, first):
            self.pass_on(h, first, 0, 1, fwd)
            self.pass_on(h, first, 0, 1, bwd)

        def start(self):
            for h in range(2):
                self.pass_on(h, 0, 0, 0, fwd)
                self.pass_on(h, 0, 0, 0, bwd)
            for h in range(2):
                self.turn(h, 0)

        def round(self, number):
            for first, second in order[number]:
                for h in range(2):
                    place = slot(h, first, second)
                    arrived(self.piece(h, place), row_sem.at[self.stage, self.g, h, place])
                    if second == 0:
                        if first == 1:
                            self.pass_on(h, 1, 0, 0, fwd)
                        self.turn(h, first)
                    elif second == 1:
                        self.pass_on(h, first, 1, 1, fwd)

    class Ring:
        def __init__(self, piece, own, shared):
            self.piece, self.own, self.shared = piece, own, shared

        def at(self, core, away, lane_sign):
            return self.piece(lax.rem(z - lane_sign * away + 8, 4) * 2 + core)

        def have(self, away):
            here = self.at(p, away, sign)
            for n, direction in ((1, fwd), (3, bwd)):
                if away == 0 or (away == 1 and n == 1):
                    send(here, here, self.own.at[(away + n) % 4], direction["z"])
            send(here, here, self.shared.at[away], sibling)

        def take(self, *aways):
            for away in aways:
                arrived(self.at(p, away, sign), self.own.at[away])
                self.have(away)

        def finish(self):
            for away in range(4):
                arrived(self.at(1 - p, away, -sign), self.shared.at[away])

    def column_ring(stage, g, col):
        return Ring(lambda source: col.at[2 * source + g], col_sem.at[stage, g], sib_sem.at[stage, g])

    def move_ring(g):
        return Ring(
            lambda source: moved.at[pl.ds(source * per + g * per_group, per_group)],
            end_sem.at[g], end_sib_sem.at[g],
        )

    def multiply(g, row, *pairs):
        here = pl.ds(g * group, group)
        for total, _ in pairs:
            total[here, :] = jnp.zeros((group, cols), F32)

        def one(place, carry):
            behind_y, behind_x = place // 4, place % 4
            k = lax.rem(y - sign * behind_y + 8, 4) * 4 + lax.rem(x - sign * behind_x + 8, 4)
            for total, col in pairs:
                total[here, :] += jnp.dot(row[g, place], col[k], preferred_element_type=F32)
            return carry

        lax.fori_loop(0, 16, one, 0)

    def fold(v):
        return jnp.sum(v.reshape(bs // 8, 8, bs), axis=0)

    totals = [jnp.zeros((8, bs), F32)] * 3

    def make_square(g):
        multiply(g, row_c, (square, col_c))
        for i in range(g * per_group, (g + 1) * per_group):
            for j in range(3):
                value = square[block(i, j)] * kept(i, j)
                square[block(i, j)] = value
                rounded = value.astype(BF16)
                inner = i - g * per_group
                row_s[(g, 0) + block(inner, j)] = rounded
                col_s[(2 * r + g,) + block(inner, j)] = rounded

    def add_sums(g):
        for i in range(g * per_group, (g + 1) * per_group):
            for j in range(3):
                inner = i - g * per_group
                value = square[block(i, j)]
                difference = dens[block(i, j)] * kept(i, j) - value
                wide = row_s[(g, 0) + block(inner, j)].astype(F32)
                one = row_c[(g, 0) + block(inner, j)].astype(F32)
                terms = (wide * one, wide * wide, difference * difference)
                for n, v in enumerate(terms):
                    totals[n] = totals[n] + fold(v)

    def reduce_start(n):
        for k, device in enumerate(reduce_peers[n]):
            send(sums.at[n], sums_in.at[n, k], sum_sem.at[n, k], device)

    def reduce_end(n):
        total = sums[n]
        for k in range(len(reduce_peers[n])):
            arrived(sums_in.at[n, k], sum_sem.at[n, k])
            total += sums_in[n, k]
        sums[n + 1] = total

    def make_result(g):
        multiply(g, row_s, (cubic, col_c), (quartic, col_s))
        trace_cubic, trace_quartic, spread = (
            jnp.sum(sums[3, n], keepdims=True) for n in range(3)
        )
        electrons = F32(rows * 8 // 2)
        factor = (electrons - (4.0 * trace_cubic - 3.0 * trace_quartic)) / (spread + 1e-06)
        for i in range(g * per_group, (g + 1) * per_group):
            for j in range(3):
                three, four = cubic[block(i, j)], quartic[block(i, j)]
                value = 4.0 * three - 3.0 * four + factor * (square[block(i, j)] - 2.0 * three + four)
                moved[r * per + i, :, j * bs:(j + 1) * bs] = (value * kept(i, j)).astype(BF16)

    c0, c1 = (Rows(0, g, row_c) for g in range(2))
    s0, s1 = (Rows(1, g, row_s) for g in range(2))
    zc0, zc1 = (column_ring(0, g, col_c) for g in range(2))
    zs0, zs1 = (column_ring(1, g, col_s) for g in range(2))
    m0, m1 = (move_ring(g) for g in range(2))

    c0.start()
    zc0.have(0)
    zc1.have(0)
    c0.round(0)
    zc0.take(1, 3)
    c0.round(1)
    zc1.take(1, 3)
    c0.round(2)
    zc0.take(2)
    c1.start()
    c0.round(3)
    zc1.take(2)
    zc0.finish()
    zc1.finish()
    c0.round(4)
    c1.round(0)
    c0.round(5)
    c1.round(1)
    c0.round(6)
    make_square(0)
    zs0.have(0)
    c1.round(2)
    s0.start()
    c1.round(3)
    add_sums(0)
    c1.round(4)
    zs0.take(1, 3)
    s0.round(0)
    c1.round(5)
    c1.round(6)
    make_square(1)
    zs1.have(0)
    add_sums(1)
    for n in range(3):
        sums[0, n] = totals[n]
    reduce_start(0)
    zs0.take(2)
    s0.round(1)
    reduce_end(0)
    reduce_start(1)
    s0.round(2)
    zs1.take(1, 3)
    s1.start()
    reduce_end(1)
    reduce_start(2)
    s0.round(3)
    zs1.take(2)
    zs0.finish()
    zs1.finish()
    s0.round(4)
    reduce_end(2)
    s1.round(0)
    s0.round(5)
    s1.round(1)
    s0.round(6)
    make_result(0)
    m0.have(0)
    s1.round(2)
    s1.round(3)
    m0.take(1, 3)
    s1.round(4)
    s1.round(5)
    m0.take(2)
    s1.round(6)
    make_result(1)
    m1.have(0)

    slots = out.shape[0] // bs

    def place(i, state):
        count, sources = state
        mine = jnp.where(owner[i] == r, 1, 0)
        sources = tuple(
            jnp.where((mine == 1) & (count == s), i, v) for s, v in enumerate(sources)
        )
        return count + mine, sources

    count, sources = lax.fori_loop(
        0, 8 * per, place, (jnp.int32(0), (jnp.int32(0),) * slots)
    )
    m1.take(1, 3, 2)
    m0.finish()
    m1.finish()
    for s in range(slots):
        found = moved[sources[s]]
        out[s * bs:(s + 1) * bs, :] = jnp.where(s < count, found, jnp.zeros_like(found))
    for copy in started:
        copy.wait_send()


def dense_step(density, keep_mask, owner_map):
    rows, cols = density.shape
    group, bs = rows // 2, cols // 3
    per = rows // bs
    dma = pltpu.SemaphoreType.DMA
    return pl.pallas_call(
        dense_kernel,
        out_shape=jax.ShapeDtypeStruct(((per + 2) * bs, cols), BF16),
        in_specs=[
            pl.BlockSpec(memory_space=pltpu.VMEM),
            pl.BlockSpec(memory_space=pltpu.SMEM),
            pl.BlockSpec(memory_space=pltpu.SMEM),
        ],
        out_specs=pl.BlockSpec(memory_space=pltpu.VMEM),
        scratch_shapes=[
            pltpu.VMEM((2, 16, group, cols), BF16),
            pltpu.VMEM((2, 16, group, cols), BF16),
            pltpu.VMEM((16, group, cols), BF16),
            pltpu.VMEM((16, group, cols), BF16),
            pltpu.VMEM((rows, cols), F32),
            pltpu.VMEM((rows, cols), F32),
            pltpu.VMEM((rows, cols), F32),
            pltpu.VMEM((8 * per, bs, cols), BF16),
            pltpu.VMEM((4, 3, 8, bs), F32),
            pltpu.VMEM((3, 7, 3, 8, bs), F32),
            dma((180,)),
            dma((2, 2, 2, 16)),
            dma((2, 2, 4)),
            dma((2, 2, 4)),
            dma((2, 4)),
            dma((2, 4)),
            dma((3, 7)),
        ],
        compiler_params=pltpu.CompilerParams(
            collective_id=1, has_side_effects=True, vmem_limit_bytes=56 << 20
        ),
    )(density, keep_mask, owner_map)


LIST = 7
BUNDLE = 18


def packed_kernel(
    dens, keep, owner, out,
    blocks, col_c, col_s, left, square, cubic, quartic, moved, sums, sums_in, spots, spots_here, counts, offsets,
    send_sem, row_sem, col_sem, sib_sem, end_sem, end_sib_sem, sum_sem, *lists,
):
    rows, cols = dens.shape
    bs = cols // 3
    per = rows // bs
    tile = per * 3
    part = tile // 2

    def origin(i):
        return i % (per // 2) * 2 + i // (per // 2)

    list_c, list_s = lists[0:2], lists[2:4]
    bundle_c, bundle_s = (lists[4:8], lists[8:12]), (lists[12:16], lists[16:20])
    r = lax.axis_index("row")
    c = lax.axis_index("col")
    z, p = r // 2, r % 2
    y, x = c // 4, c % 4
    sign = 1 - 2 * p

    def at(dz=0, dp=0, dy=0, dx=0):
        return (
            lax.rem(z + dz + 4, 4) * 2 + lax.rem(p + dp, 2),
            lax.rem(y + dy + 4, 4) * 4 + lax.rem(x + dx + 4, 4),
        )

    sibling = at(dp=1)
    fwd = {"x": at(dx=sign), "y": at(dy=sign), "z": at(dz=sign)}
    bwd = {"x": at(dx=-sign), "y": at(dy=-sign), "z": at(dz=-sign)}
    reduce_peers = (
        [at(dz=k // 2, dp=k % 2) for k in range(1, 8)],
        [at(dy=k // 4, dx=k % 4) for k in range(1, 16)],
    )

    barrier = pltpu.get_barrier_semaphore()
    for devices in reduce_peers:
        for device in devices:
            pl.semaphore_signal(barrier, inc=1, device_id=device, device_id_type=MESH)

    def block(i, j):
        return (slice(i * bs, (i + 1) * bs), slice(j * bs, (j + 1) * bs))

    def kept(i, j):
        return keep[r * per + origin(i), c * 3 + j].astype(F32)

    def col_block(i, j):
        return (2 * r + origin(i) // (per // 2),) + block(origin(i) % (per // 2), j)

    for i in range(per):
        for j in range(3):
            value = (dens[block(origin(i), j)] * kept(i, j)).astype(BF16)
            blocks[i * 3 + j] = value
            col_c[col_block(i, j)] = value

    def find(h):
        count, sources = jnp.int32(0), [jnp.int32(h * part)] * LIST
        for b in range(h * part, (h + 1) * part):
            one = keep[r * per + origin(b // 3), c * 3 + b % 3]
            sources = [
                jnp.where((one == 1) & (count == s), b, v) for s, v in enumerate(sources)
            ]
            count = count + one
        return sources

    listed = [find(0), find(1)]

    def pack(targets):
        for h in range(2):
            for s in range(LIST):
                targets[h][s] = blocks[listed[h][s]]

    pack(list_c)
    pl.semaphore_wait(barrier, sum(len(devices) for devices in reduce_peers))

    started = []

    def send(src, dst, recv, device):
        copy = pltpu.make_async_remote_copy(
            src_ref=src, dst_ref=dst, send_sem=send_sem.at[len(started)],
            recv_sem=recv, device_id=device, device_id_type=MESH,
        )
        copy.start()
        started.append(copy)

    def arrived(dst, recv):
        pltpu.make_async_remote_copy(
            src_ref=dst, dst_ref=dst, send_sem=send_sem.at[0],
            recv_sem=recv, device_id=sibling, device_id_type=MESH,
        ).wait_recv()

    pending = []

    def work(count):
        for _ in range(min(count, len(pending))):
            pending.pop(0)()

    routes = (("x", "y"), ("y", "x"))

    class Rows:
        def __init__(self, stage, lists, bundles, ready):
            self.stage, self.lists, self.bundles, self.ready = stage, lists, bundles, ready

        def piece(self, ring, h, away):
            if ring == 0:
                return self.lists[h].at[pl.ds(away * LIST, LIST)]
            return self.bundles[h][away]

        def have(self, ring, h, away):
            for n, direction in ((1, fwd), (3, bwd)):
                if away == 0 or (away == 1 and n == 1):
                    goal = (away + n) % 4
                    send(
                        self.piece(ring, h, away), self.piece(ring, h, goal),
                        row_sem.at[self.stage, ring, h, goal], direction[routes[h][ring]],
                    )

        def start(self):
            for h in range(2):
                self.have(0, h, 0)

        def take(self, ring, *aways):
            for away in aways:
                for h in range(2):
                    arrived(self.piece(ring, h, away), row_sem.at[self.stage, ring, h, away])
                    self.have(ring, h, away)
                    if ring == 1:
                        self.ready(h, away)

        def bundle(self):
            for h in range(2):
                place = x if h == 0 else y
                starts = [
                    offsets[h * 16 + (4 * y + t if h == 0 else 4 * t + x)] for t in range(4)
                ]
                label = [lax.rem(sign * (place - t) + 8, 4) * LIST for t in range(4)]
                for s in range(BUNDLE):
                    shift = label[0]
                    for t in range(1, 4):
                        shift = jnp.where(s >= starts[t], label[t] - starts[t], shift)
                    source = jnp.minimum(jnp.maximum(s + shift, 0), 4 * LIST - 1)
                    self.bundles[h][0][s] = self.lists[h][source]
                self.have(1, h, 0)
                self.ready(h, 0)

    class Ring:
        def __init__(self, piece, own, shared):
            self.piece, self.own, self.shared = piece, own, shared

        def at(self, core, away, lane_sign):
            return self.piece(lax.rem(z - lane_sign * away + 8, 4) * 2 + core)

        def have(self, away):
            here = self.at(p, away, sign)
            for n, direction in ((1, fwd), (3, bwd)):
                if away == 0 or (away == 1 and n == 1):
                    send(here, here, self.own.at[(away + n) % 4], direction["z"])
            send(here, here, self.shared.at[away], sibling)

        def take(self, *aways):
            for away in aways:
                arrived(self.at(p, away, sign), self.own.at[away])
                self.have(away)

        def finish(self):
            for away in range(4):
                arrived(self.at(1 - p, away, -sign), self.shared.at[away])

    def columns(stage, col):
        return Ring(lambda source: col.at[pl.ds(2 * source, 2)], col_sem.at[stage], sib_sem.at[stage])

    def column_of(place):
        behind_y, behind_x = divmod(place, 4)
        return lax.rem(y - sign * behind_y + 8, 4) * 4 + lax.rem(x - sign * behind_x + 8, 4)

    def spread(bundles, h, place):
        source = column_of(place)
        start = offsets[h * 16 + source]
        bundle = bundles[h][place // 4 if h == 0 else place % 4]
        for i in range(h * per // 2, (h + 1) * per // 2):
            for j in range(3):
                spot = jnp.minimum(start + spots[source * tile + i * 3 + j], BUNDLE - 1)
                found = bundle[spot]
                there = keep[r * per + origin(i), source * 3 + j] == 1
                left[block(i, j)] = jnp.where(there, found, jnp.zeros_like(found))

    fresh = set()

    def add(name, total, h, place, col):
        here = pl.ds(h * (rows // 2), rows // 2)
        term = jnp.dot(left[here, :], col[column_of(place)], preferred_element_type=F32)
        if (name, h) in fresh:
            total[here, :] += term
        else:
            fresh.add((name, h))
            total[here, :] = term

    waiting = []
    columns_ready = []

    def first_product(h, place):
        spread(bundle_c, h, place)
        add("square", square, h, place, col_c)

    def second_product(h, place):
        spread(bundle_s, h, place)
        add("cubic", cubic, h, place, col_c)
        add("quartic", quartic, h, place, col_s)

    def ready_for(product):
        def ready(h, away):
            for other in range(4):
                place = 4 * away + other if h == 0 else 4 * other + away
                waiting.append(lambda place=place: product(h, place))
            if columns_ready:
                pending.extend(waiting)
                waiting.clear()
        return ready

    def now_columns():
        columns_ready.append(True)
        pending.extend(waiting)
        waiting.clear()

    rows_c = Rows(0, list_c, bundle_c, ready_for(first_product))
    rows_s = Rows(1, list_s, bundle_s, ready_for(second_product))
    ring_c, ring_s = columns(0, col_c), columns(1, col_s)

    rows_c.start()
    ring_c.have(0)

    def number(source, carry):
        for h in range(2):
            count = jnp.int32(0)
            for b in range(h * part, (h + 1) * part):
                spots[source * tile + b] = count
                count = count + keep[r * per + origin(b // 3), source * 3 + b % 3]
            counts[2 * source + h] = count
        return carry

    lax.fori_loop(0, 16, number, 0)
    for h in range(2):
        for i in range(4):
            start = jnp.int32(0)
            for t in range(4):
                source = 4 * i + t if h == 0 else 4 * t + i
                offsets[h * 16 + source] = start
                start = start + counts[2 * source + h]

    rows_c.take(0, 1, 3, 2)
    rows_c.bundle()
    ring_c.take(1, 3)
    ring_c.take(2)
    rows_c.take(1, 1)
    ring_c.finish()
    now_columns()
    work(12)
    rows_c.take(1, 3)
    work(len(pending))
    rows_c.take(1, 2)
    work(len(pending))
    columns_ready.clear()

    for i in range(per):
        for j in range(3):
            value = square[block(i, j)] * kept(i, j)
            square[block(i, j)] = value
            rounded = value.astype(BF16)
            col_s[col_block(i, j)] = rounded
            blocks[i * 3 + j] = rounded
    pack(list_s)
    rows_s.start()
    ring_s.have(0)

    def fold(v):
        return jnp.sum(v.reshape(bs // 8, 8, bs), axis=0)

    totals = [jnp.zeros((8, bs), F32)] * 3
    for i in range(per):
        for j in range(3):
            value = square[block(i, j)]
            difference = dens[block(origin(i), j)] * kept(i, j) - value
            wide = blocks[i * 3 + j].astype(F32)
            one = col_c[col_block(i, j)].astype(F32)
            terms = (wide * one, wide * wide, difference * difference)
            totals = [t + fold(v) for t, v in zip(totals, terms, strict=True)]
    sums[0] = jnp.zeros((8, bs), F32)
    for n in range(3):
        sums[0, n:n + 1] = jnp.sum(totals[n], axis=0, keepdims=True)

    def reduce_start(n):
        for k, device in enumerate(reduce_peers[n]):
            send(sums.at[n], sums_in.at[n, k], sum_sem.at[n, k], device)

    def reduce_end(n):
        total = sums[n]
        for k in range(len(reduce_peers[n])):
            arrived(sums_in.at[n, k], sum_sem.at[n, k])
            total += sums_in[n, k]
        sums[n + 1] = total

    reduce_start(0)
    rows_s.take(0, 1, 3, 2)
    rows_s.bundle()
    ring_s.take(1, 3)
    ring_s.take(2)
    rows_s.take(1, 1)
    reduce_end(0)
    reduce_start(1)
    ring_s.finish()
    now_columns()
    work(8)
    rows_s.take(1, 3)
    work(len(pending))
    rows_s.take(1, 2)
    work(len(pending))
    reduce_end(1)

    trace_cubic, trace_quartic, spread_sum = (
        jnp.sum(sums[2, n:n + 1], keepdims=True) for n in range(3)
    )
    electrons = F32(rows * 8 // 2)
    factor = (electrons - (4.0 * trace_cubic - 3.0 * trace_quartic)) / (spread_sum + 1e-06)
    for i in range(per):
        for j in range(3):
            three, four = cubic[block(i, j)], quartic[block(i, j)]
            value = 4.0 * three - 3.0 * four + factor * (square[block(i, j)] - 2.0 * three + four)
            blocks[i * 3 + j] = (value * kept(i, j)).astype(BF16)
    for h in range(2):
        for s in range(LIST):
            moved[(2 * r + h) * LIST + s] = blocks[listed[h][s]]
    ring_t = Ring(lambda source: moved.at[pl.ds(2 * source * LIST, 2 * LIST)], end_sem, end_sib_sem)
    ring_t.have(0)

    slots = out.shape[0] // bs

    def number_here(source, carry):
        for h in range(2):
            count = jnp.int32(0)
            for b in range(h * part, (h + 1) * part):
                spots_here[source * tile + b] = jnp.minimum(count, LIST - 1) + (2 * source + h) * LIST
                count = count + keep[source * per + origin(b // 3), c * 3 + b % 3]
        return carry

    lax.fori_loop(0, 8, number_here, 0)

    def place_rows(i, state):
        count, sources = state
        one = jnp.where(owner[i] == r, 1, 0)
        sources = tuple(
            jnp.where((one == 1) & (count == s), i, v) for s, v in enumerate(sources)
        )
        return count + one, sources

    count, sources = lax.fori_loop(
        0, 8 * per, place_rows, (jnp.int32(0), (jnp.int32(0),) * slots)
    )
    ring_t.take(1, 3, 2)
    ring_t.finish()
    for s in range(slots):
        for j in range(3):
            inner = sources[s] % per
            at_place = sources[s] - inner + inner % 2 * (per // 2) + inner // 2
            found = moved[spots_here[at_place * 3 + j]]
            there = (s < count) & (keep[sources[s], c * 3 + j] == 1)
            out[block(s, j)] = jnp.where(there, found, jnp.zeros_like(found))
    for copy in started:
        copy.wait_send()


def packed_step(density, keep_mask, owner_map):
    rows, cols = density.shape
    bs = cols // 3
    per = rows // bs
    dma = pltpu.SemaphoreType.DMA
    return pl.pallas_call(
        packed_kernel,
        out_shape=jax.ShapeDtypeStruct(((per + 2) * bs, cols), BF16),
        in_specs=[
            pl.BlockSpec(memory_space=pltpu.VMEM),
            pl.BlockSpec(memory_space=pltpu.SMEM),
            pl.BlockSpec(memory_space=pltpu.SMEM),
        ],
        out_specs=pl.BlockSpec(memory_space=pltpu.VMEM),
        scratch_shapes=[
            pltpu.VMEM((per * 3, bs, bs), BF16),
            pltpu.VMEM((16, cols, cols), BF16),
            pltpu.VMEM((16, cols, cols), BF16),
            pltpu.VMEM((rows, cols), BF16),
            pltpu.VMEM((rows, cols), F32),
            pltpu.VMEM((rows, cols), F32),
            pltpu.VMEM((rows, cols), F32),
            pltpu.VMEM((16 * LIST, bs, bs), BF16),
            pltpu.VMEM((3, 8, bs), F32),
            pltpu.VMEM((2, 15, 8, bs), F32),
            pltpu.SMEM((16 * per * 3,), jnp.int32),
            pltpu.SMEM((8 * per * 3,), jnp.int32),
            pltpu.SMEM((32,), jnp.int32),
            pltpu.SMEM((32,), jnp.int32),
            dma((108,)),
            dma((2, 2, 2, 4)),
            dma((2, 4)),
            dma((2, 4)),
            dma((4,)),
            dma((4,)),
            dma((2, 15)),
        ] + [pltpu.VMEM((4 * LIST, bs, bs), BF16)] * 4 + [pltpu.VMEM((BUNDLE, bs, bs), BF16)] * 16,
        compiler_params=pltpu.CompilerParams(
            collective_id=0, has_side_effects=True, vmem_limit_bytes=56 << 20
        ),
    )(density, keep_mask, owner_map)


def step(density, keep_mask, owner_map):
    rows = lax.axis_size("row")
    blocks = keep_mask.shape[0]
    halves = keep_mask.reshape(rows, blocks // rows // 2, 2, 4, 4, 3).sum(axis=(1, 5))
    upper, lower = halves[:, 0], halves[:, 1]
    excess = jnp.maximum(
        jnp.maximum(upper, lower) - LIST,
        jnp.maximum(upper.sum(axis=2, keepdims=True), lower.sum(axis=1, keepdims=True)) - BUNDLE,
    )
    return lax.cond(
        jnp.max(excess) <= 0, packed_step, dense_step, density, keep_mask, owner_map
    ).astype(F32)


def solution(mesh):
    return jax.shard_map(
        step,
        mesh=mesh,
        in_specs=(P("row", "col"), P(), P()),
        out_specs=P("row", "col"),
        check_vma=False,
    )
```

```python
import jax
import jax.numpy as jnp
from jax import lax
from jax.experimental import pallas as pl
from jax.experimental.pallas import tpu as pltpu
from jax.sharding import PartitionSpec as P

MESH = pl.DeviceIdType.MESH
F32 = jnp.float32
BF16 = jnp.bfloat16


def dense_kernel(
    dens, keep, owner, out,
    row_c, row_s, col_c, col_s, square, cubic, quartic, moved, sums, sums_in,
    send_sem, row_sem, col_sem, sib_sem, end_sem, end_sib_sem, sum_sem,
):
    rows, cols = dens.shape
    group = rows // 2
    half = group // 2
    r = lax.axis_index("row")
    c = lax.axis_index("col")
    z, p = r // 2, r % 2
    y, x = c // 4, c % 4
    sign = 1 - 2 * p
    bs = cols // 3
    per = rows // bs
    per_group = per // 2

    def at(dz=0, dp=0, dy=0, dx=0):
        return (
            lax.rem(z + dz + 4, 4) * 2 + lax.rem(p + dp, 2),
            lax.rem(y + dy + 4, 4) * 4 + lax.rem(x + dx + 4, 4),
        )

    sibling = at(dp=1)
    fwd = {"x": at(dx=sign), "y": at(dy=sign), "z": at(dz=sign)}
    bwd = {"x": at(dx=-sign), "y": at(dy=-sign), "z": at(dz=-sign)}
    reduce_peers = (
        [at(dz=k // 2, dp=k % 2) for k in range(1, 8)],
        [at(dx=k) for k in range(1, 4)],
        [at(dy=k) for k in range(1, 4)],
    )

    barrier = pltpu.get_barrier_semaphore()
    for devices in reduce_peers:
        for device in devices:
            pl.semaphore_signal(barrier, inc=1, device_id=device, device_id_type=MESH)

    def block(i, j):
        return (slice(i * bs, (i + 1) * bs), slice(j * bs, (j + 1) * bs))

    def kept(i, j):
        return keep[r * per + i, c * 3 + j].astype(F32)

    for i in range(per):
        for j in range(3):
            value = (dens[block(i, j)] * kept(i, j)).astype(BF16)
            g, inner = divmod(i, per_group)
            row_c[(g, 0) + block(inner, j)] = value
            col_c[(2 * r + g,) + block(inner, j)] = value

    pl.semaphore_wait(barrier, sum(len(devices) for devices in reduce_peers))

    started = []

    def send(src, dst, recv, device):
        copy = pltpu.make_async_remote_copy(
            src_ref=src, dst_ref=dst, send_sem=send_sem.at[len(started)],
            recv_sem=recv, device_id=device, device_id_type=MESH,
        )
        copy.start()
        started.append(copy)

    def arrived(dst, recv):
        pltpu.make_async_remote_copy(
            src_ref=dst, dst_ref=dst, send_sem=send_sem.at[0],
            recv_sem=recv, device_id=sibling, device_id_type=MESH,
        ).wait_recv()

    order = (
        ((1, 0), (3, 0)),
        ((0, 1), (0, 3)),
        ((2, 0),),
        ((1, 1), (3, 1), (1, 3), (3, 3)),
        ((0, 2), (2, 1), (2, 3)),
        ((1, 2), (3, 2)),
        ((2, 2),),
    )
    routes = (("x", "y"), ("y", "x"))

    def slot(h, first, second):
        return 4 * second + first if h == 0 else 4 * first + second

    class Rows:
        def __init__(self, stage, g, row):
            self.stage, self.g, self.row = stage, g, row

        def piece(self, h, place):
            return self.row.at[self.g, place, pl.ds(h * half, half)]

        def pass_on(self, h, first, second, which, direction):
            n = 1 if direction is fwd else 3
            there = ((first + n) % 4, second) if which == 0 else (first, (second + n) % 4)
            goal = slot(h, *there)
            send(
                self.piece(h, slot(h, first, second)), self.piece(h, goal),
                row_sem.at[self.stage, self.g, h, goal], direction[routes[h][which]],
            )

        def turn(self, h, first):
            self.pass_on(h, first, 0, 1, fwd)
            self.pass_on(h, first, 0, 1, bwd)

        def start(self):
            for h in range(2):
                self.pass_on(h, 0, 0, 0, fwd)
                self.pass_on(h, 0, 0, 0, bwd)
            for h in range(2):
                self.turn(h, 0)

        def round(self, number):
            for first, second in order[number]:
                for h in range(2):
                    place = slot(h, first, second)
                    arrived(self.piece(h, place), row_sem.at[self.stage, self.g, h, place])
                    if second == 0:
                        if first == 1:
                            self.pass_on(h, 1, 0, 0, fwd)
                        self.turn(h, first)
                    elif second == 1:
                        self.pass_on(h, first, 1, 1, fwd)

    class Ring:
        def __init__(self, piece, own, shared):
            self.piece, self.own, self.shared = piece, own, shared

        def at(self, core, away, lane_sign):
            return self.piece(lax.rem(z - lane_sign * away + 8, 4) * 2 + core)

        def have(self, away):
            here = self.at(p, away, sign)
            for n, direction in ((1, fwd), (3, bwd)):
                if away == 0 or (away == 1 and n == 1):
                    send(here, here, self.own.at[(away + n) % 4], direction["z"])
            send(here, here, self.shared.at[away], sibling)

        def take(self, *aways):
            for away in aways:
                arrived(self.at(p, away, sign), self.own.at[away])
                self.have(away)

        def finish(self):
            for away in range(4):
                arrived(self.at(1 - p, away, -sign), self.shared.at[away])

    def column_ring(stage, g, col):
        return Ring(lambda source: col.at[2 * source + g], col_sem.at[stage, g], sib_sem.at[stage, g])

    def move_ring(g):
        return Ring(
            lambda source: moved.at[pl.ds(source * per + g * per_group, per_group)],
            end_sem.at[g], end_sib_sem.at[g],
        )

    def multiply(g, row, *pairs):
        here = pl.ds(g * group, group)
        for total, _ in pairs:
            total[here, :] = jnp.zeros((group, cols), F32)

        def one(place, carry):
            behind_y, behind_x = place // 4, place % 4
            k = lax.rem(y - sign * behind_y + 8, 4) * 4 + lax.rem(x - sign * behind_x + 8, 4)
            for total, col in pairs:
                total[here, :] += jnp.dot(row[g, place], col[k], preferred_element_type=F32)
            return carry

        lax.fori_loop(0, 16, one, 0)

    def fold(v):
        return jnp.sum(v.reshape(bs // 8, 8, bs), axis=0)

    totals = [jnp.zeros((8, bs), F32)] * 3

    def make_square(g):
        multiply(g, row_c, (square, col_c))
        for i in range(g * per_group, (g + 1) * per_group):
            for j in range(3):
                value = square[block(i, j)] * kept(i, j)
                square[block(i, j)] = value
                rounded = value.astype(BF16)
                inner = i - g * per_group
                row_s[(g, 0) + block(inner, j)] = rounded
                col_s[(2 * r + g,) + block(inner, j)] = rounded

    def add_sums(g):
        for i in range(g * per_group, (g + 1) * per_group):
            for j in range(3):
                inner = i - g * per_group
                value = square[block(i, j)]
                difference = dens[block(i, j)] * kept(i, j) - value
                wide = row_s[(g, 0) + block(inner, j)].astype(F32)
                one = row_c[(g, 0) + block(inner, j)].astype(F32)
                terms = (wide * one, wide * wide, difference * difference)
                for n, v in enumerate(terms):
                    totals[n] = totals[n] + fold(v)

    def reduce_start(n):
        for k, device in enumerate(reduce_peers[n]):
            send(sums.at[n], sums_in.at[n, k], sum_sem.at[n, k], device)

    def reduce_end(n):
        total = sums[n]
        for k in range(len(reduce_peers[n])):
            arrived(sums_in.at[n, k], sum_sem.at[n, k])
            total += sums_in[n, k]
        sums[n + 1] = total

    def make_result(g):
        multiply(g, row_s, (cubic, col_c), (quartic, col_s))
        trace_cubic, trace_quartic, spread = (
            jnp.sum(sums[3, n], keepdims=True) for n in range(3)
        )
        electrons = F32(rows * 8 // 2)
        factor = (electrons - (4.0 * trace_cubic - 3.0 * trace_quartic)) / (spread + 1e-06)
        for i in range(g * per_group, (g + 1) * per_group):
            for j in range(3):
                three, four = cubic[block(i, j)], quartic[block(i, j)]
                value = 4.0 * three - 3.0 * four + factor * (square[block(i, j)] - 2.0 * three + four)
                moved[r * per + i, :, j * bs:(j + 1) * bs] = (value * kept(i, j)).astype(BF16)

    c0, c1 = (Rows(0, g, row_c) for g in range(2))
    s0, s1 = (Rows(1, g, row_s) for g in range(2))
    zc0, zc1 = (column_ring(0, g, col_c) for g in range(2))
    zs0, zs1 = (column_ring(1, g, col_s) for g in range(2))
    m0, m1 = (move_ring(g) for g in range(2))

    c0.start()
    zc0.have(0)
    zc1.have(0)
    c0.round(0)
    zc0.take(1, 3)
    c0.round(1)
    zc1.take(1, 3)
    c0.round(2)
    zc0.take(2)
    c1.start()
    c0.round(3)
    zc1.take(2)
    zc0.finish()
    zc1.finish()
    c0.round(4)
    c1.round(0)
    c0.round(5)
    c1.round(1)
    c0.round(6)
    make_square(0)
    zs0.have(0)
    c1.round(2)
    s0.start()
    c1.round(3)
    add_sums(0)
    c1.round(4)
    zs0.take(1, 3)
    s0.round(0)
    c1.round(5)
    c1.round(6)
    make_square(1)
    zs1.have(0)
    add_sums(1)
    for n in range(3):
        sums[0, n] = totals[n]
    reduce_start(0)
    zs0.take(2)
    s0.round(1)
    reduce_end(0)
    reduce_start(1)
    s0.round(2)
    zs1.take(1, 3)
    s1.start()
    reduce_end(1)
    reduce_start(2)
    s0.round(3)
    zs1.take(2)
    zs0.finish()
    zs1.finish()
    s0.round(4)
    reduce_end(2)
    s1.round(0)
    s0.round(5)
    s1.round(1)
    s0.round(6)
    make_result(0)
    m0.have(0)
    s1.round(2)
    s1.round(3)
    m0.take(1, 3)
    s1.round(4)
    s1.round(5)
    m0.take(2)
    s1.round(6)
    make_result(1)
    m1.have(0)

    slots = out.shape[0] // bs

    def place(i, state):
        count, sources = state
        mine = jnp.where(owner[i] == r, 1, 0)
        sources = tuple(
            jnp.where((mine == 1) & (count == s), i, v) for s, v in enumerate(sources)
        )
        return count + mine, sources

    count, sources = lax.fori_loop(
        0, 8 * per, place, (jnp.int32(0), (jnp.int32(0),) * slots)
    )
    m1.take(1, 3, 2)
    m0.finish()
    m1.finish()
    for s in range(slots):
        found = moved[sources[s]]
        out[s * bs:(s + 1) * bs, :] = jnp.where(s < count, found, jnp.zeros_like(found))
    for copy in started:
        copy.wait_send()


def dense_step(density, keep_mask, owner_map):
    rows, cols = density.shape
    group, bs = rows // 2, cols // 3
    per = rows // bs
    dma = pltpu.SemaphoreType.DMA
    return pl.pallas_call(
        dense_kernel,
        out_shape=jax.ShapeDtypeStruct(((per + 2) * bs, cols), BF16),
        in_specs=[
            pl.BlockSpec(memory_space=pltpu.VMEM),
            pl.BlockSpec(memory_space=pltpu.SMEM),
            pl.BlockSpec(memory_space=pltpu.SMEM),
        ],
        out_specs=pl.BlockSpec(memory_space=pltpu.VMEM),
        scratch_shapes=[
            pltpu.VMEM((2, 16, group, cols), BF16),
            pltpu.VMEM((2, 16, group, cols), BF16),
            pltpu.VMEM((16, group, cols), BF16),
            pltpu.VMEM((16, group, cols), BF16),
            pltpu.VMEM((rows, cols), F32),
            pltpu.VMEM((rows, cols), F32),
            pltpu.VMEM((rows, cols), F32),
            pltpu.VMEM((8 * per, bs, cols), BF16),
            pltpu.VMEM((4, 3, 8, bs), F32),
            pltpu.VMEM((3, 7, 3, 8, bs), F32),
            dma((180,)),
            dma((2, 2, 2, 16)),
            dma((2, 2, 4)),
            dma((2, 2, 4)),
            dma((2, 4)),
            dma((2, 4)),
            dma((3, 7)),
        ],
        compiler_params=pltpu.CompilerParams(
            collective_id=1, has_side_effects=True, vmem_limit_bytes=56 << 20
        ),
    )(density, keep_mask, owner_map)


LIST = 7
BUNDLE = 18


def packed_kernel(
    dens, keep, owner, out,
    blocks, col_c, col_s, left, square, cubic, quartic, moved, sums, sums_in, spots, spots_here, counts, offsets,
    send_sem, row_sem, col_sem, sib_sem, end_sem, end_sib_sem, sum_sem, *lists,
):
    rows, cols = dens.shape
    bs = cols // 3
    per = rows // bs
    tile = per * 3
    part = tile // 2

    def origin(i):
        return i % (per // 2) * 2 + i // (per // 2)

    list_c, list_s = lists[0:2], lists[2:4]
    bundle_c, bundle_s = (lists[4:8], lists[8:12]), (lists[12:16], lists[16:20])
    r = lax.axis_index("row")
    c = lax.axis_index("col")
    z, p = r // 2, r % 2
    y, x = c // 4, c % 4
    sign = 1 - 2 * p

    def at(dz=0, dp=0, dy=0, dx=0):
        return (
            lax.rem(z + dz + 4, 4) * 2 + lax.rem(p + dp, 2),
            lax.rem(y + dy + 4, 4) * 4 + lax.rem(x + dx + 4, 4),
        )

    sibling = at(dp=1)
    fwd = {"x": at(dx=sign), "y": at(dy=sign), "z": at(dz=sign)}
    bwd = {"x": at(dx=-sign), "y": at(dy=-sign), "z": at(dz=-sign)}
    reduce_peers = (
        [at(dz=k // 2, dp=k % 2) for k in range(1, 8)],
        [at(dy=k // 4, dx=k % 4) for k in range(1, 16)],
    )

    barrier = pltpu.get_barrier_semaphore()
    for devices in reduce_peers:
        for device in devices:
            pl.semaphore_signal(barrier, inc=1, device_id=device, device_id_type=MESH)

    def block(i, j):
        return (slice(i * bs, (i + 1) * bs), slice(j * bs, (j + 1) * bs))

    def kept(i, j):
        return keep[r * per + origin(i), c * 3 + j].astype(F32)

    def col_block(i, j):
        return (2 * r + origin(i) // (per // 2),) + block(origin(i) % (per // 2), j)

    for i in range(per):
        for j in range(3):
            value = (dens[block(origin(i), j)] * kept(i, j)).astype(BF16)
            blocks[i * 3 + j] = value
            col_c[col_block(i, j)] = value

    def find(h):
        count, sources = jnp.int32(0), [jnp.int32(h * part)] * LIST
        for b in range(h * part, (h + 1) * part):
            one = keep[r * per + origin(b // 3), c * 3 + b % 3]
            sources = [
                jnp.where((one == 1) & (count == s), b, v) for s, v in enumerate(sources)
            ]
            count = count + one
        return sources

    listed = [find(0), find(1)]

    def pack(targets):
        for h in range(2):
            for s in range(LIST):
                targets[h][s] = blocks[listed[h][s]]

    pack(list_c)
    pl.semaphore_wait(barrier, sum(len(devices) for devices in reduce_peers))

    started = []

    def send(src, dst, recv, device):
        copy = pltpu.make_async_remote_copy(
            src_ref=src, dst_ref=dst, send_sem=send_sem.at[len(started)],
            recv_sem=recv, device_id=device, device_id_type=MESH,
        )
        copy.start()
        started.append(copy)

    def arrived(dst, recv):
        pltpu.make_async_remote_copy(
            src_ref=dst, dst_ref=dst, send_sem=send_sem.at[0],
            recv_sem=recv, device_id=sibling, device_id_type=MESH,
        ).wait_recv()

    pending = []

    def work(count):
        for _ in range(min(count, len(pending))):
            pending.pop(0)()

    routes = (("x", "y"), ("y", "x"))

    class Rows:
        def __init__(self, stage, lists, bundles, ready):
            self.stage, self.lists, self.bundles, self.ready = stage, lists, bundles, ready

        def piece(self, ring, h, away):
            if ring == 0:
                return self.lists[h].at[pl.ds(away * LIST, LIST)]
            return self.bundles[h][away]

        def have(self, ring, h, away):
            for n, direction in ((1, fwd), (3, bwd)):
                if away == 0 or (away == 1 and n == 1):
                    goal = (away + n) % 4
                    send(
                        self.piece(ring, h, away), self.piece(ring, h, goal),
                        row_sem.at[self.stage, ring, h, goal], direction[routes[h][ring]],
                    )

        def start(self):
            for h in range(2):
                self.have(0, h, 0)

        def take(self, ring, *aways):
            for away in aways:
                for h in range(2):
                    arrived(self.piece(ring, h, away), row_sem.at[self.stage, ring, h, away])
                    self.have(ring, h, away)
                    if ring == 1:
                        self.ready(h, away)

        def bundle(self):
            for h in range(2):
                place = x if h == 0 else y
                starts = [
                    offsets[h * 16 + (4 * y + t if h == 0 else 4 * t + x)] for t in range(4)
                ]
                label = [lax.rem(sign * (place - t) + 8, 4) * LIST for t in range(4)]
                for s in range(BUNDLE):
                    shift = label[0]
                    for t in range(1, 4):
                        shift = jnp.where(s >= starts[t], label[t] - starts[t], shift)
                    source = jnp.minimum(jnp.maximum(s + shift, 0), 4 * LIST - 1)
                    self.bundles[h][0][s] = self.lists[h][source]
                self.have(1, h, 0)
                self.ready(h, 0)

    class Ring:
        def __init__(self, piece, own, shared):
            self.piece, self.own, self.shared = piece, own, shared

        def at(self, core, away, lane_sign):
            return self.piece(lax.rem(z - lane_sign * away + 8, 4) * 2 + core)

        def have(self, away):
            here = self.at(p, away, sign)
            for n, direction in ((1, fwd), (3, bwd)):
                if away == 0 or (away == 1 and n == 1):
                    send(here, here, self.own.at[(away + n) % 4], direction["z"])
            send(here, here, self.shared.at[away], sibling)

        def take(self, *aways):
            for away in aways:
                arrived(self.at(p, away, sign), self.own.at[away])
                self.have(away)

        def finish(self):
            for away in range(4):
                arrived(self.at(1 - p, away, -sign), self.shared.at[away])

    def columns(stage, col):
        return Ring(lambda source: col.at[pl.ds(2 * source, 2)], col_sem.at[stage], sib_sem.at[stage])

    def spread(bundles, h, away):
        behind = lax.rem((y if h == 0 else x) - sign * away + 8, 4)
        bundle = bundles[h][away]
        sources = [4 * behind + t if h == 0 else 4 * t + behind for t in range(4)]
        for t, source in enumerate(sources):
            start = offsets[h * 16 + source]
            for i in range(per // 2):
                for j in range(3):
                    b = (h * per // 2 + i) * 3 + j
                    spot = jnp.minimum(start + spots[source * tile + b], BUNDLE - 1)
                    found = bundle[spot]
                    there = keep[r * per + origin(b // 3), source * 3 + j] == 1
                    left[block(i, 3 * t + j)] = jnp.where(there, found, jnp.zeros_like(found))
        return sources

    fresh = set()

    def add(name, total, h, sources, col):
        here = pl.ds(h * (rows // 2), rows // 2)
        if h == 0:
            right = col[pl.ds(sources[0], 4)].reshape(4 * cols, cols)
        else:
            right = jnp.concatenate([col[source] for source in sources], axis=0)
        term = jnp.dot(left[...], right, preferred_element_type=F32)
        if (name, h) in fresh:
            total[here, :] += term
        else:
            fresh.add((name, h))
            total[here, :] = term

    waiting = []
    columns_ready = []

    def first_product(h, away):
        sources = spread(bundle_c, h, away)
        add("square", square, h, sources, col_c)

    def second_product(h, away):
        sources = spread(bundle_s, h, away)
        add("cubic", cubic, h, sources, col_c)
        add("quartic", quartic, h, sources, col_s)

    def ready_for(product):
        def ready(h, away):
            waiting.append(lambda: product(h, away))
            if columns_ready:
                pending.extend(waiting)
                waiting.clear()
        return ready

    def now_columns():
        columns_ready.append(True)
        pending.extend(waiting)
        waiting.clear()

    rows_c = Rows(0, list_c, bundle_c, ready_for(first_product))
    rows_s = Rows(1, list_s, bundle_s, ready_for(second_product))
    ring_c, ring_s = columns(0, col_c), columns(1, col_s)

    rows_c.start()
    ring_c.have(0)

    def number(source, carry):
        for h in range(2):
            count = jnp.int32(0)
            for b in range(h * part, (h + 1) * part):
                spots[source * tile + b] = count
                count = count + keep[r * per + origin(b // 3), source * 3 + b % 3]
            counts[2 * source + h] = count
        return carry

    lax.fori_loop(0, 16, number, 0)
    for h in range(2):
        for i in range(4):
            start = jnp.int32(0)
            for t in range(4):
                source = 4 * i + t if h == 0 else 4 * t + i
                offsets[h * 16 + source] = start
                start = start + counts[2 * source + h]

    rows_c.take(0, 1, 3, 2)
    rows_c.bundle()
    ring_c.take(1, 3)
    ring_c.take(2)
    rows_c.take(1, 1)
    ring_c.finish()
    now_columns()
    work(3)
    rows_c.take(1, 3)
    work(len(pending))
    rows_c.take(1, 2)
    work(len(pending))
    columns_ready.clear()

    for i in range(per):
        for j in range(3):
            value = square[block(i, j)] * kept(i, j)
            square[block(i, j)] = value
            rounded = value.astype(BF16)
            col_s[col_block(i, j)] = rounded
            blocks[i * 3 + j] = rounded
    pack(list_s)
    rows_s.start()
    ring_s.have(0)

    def fold(v):
        return jnp.sum(v.reshape(bs // 8, 8, bs), axis=0)

    totals = [jnp.zeros((8, bs), F32)] * 3
    for i in range(per):
        for j in range(3):
            value = square[block(i, j)]
            difference = dens[block(origin(i), j)] * kept(i, j) - value
            wide = blocks[i * 3 + j].astype(F32)
            one = col_c[col_block(i, j)].astype(F32)
            terms = (wide * one, wide * wide, difference * difference)
            totals = [t + fold(v) for t, v in zip(totals, terms, strict=True)]
    sums[0] = jnp.zeros((8, bs), F32)
    for n in range(3):
        sums[0, n:n + 1] = jnp.sum(totals[n], axis=0, keepdims=True)

    def reduce_start(n):
        for k, device in enumerate(reduce_peers[n]):
            send(sums.at[n], sums_in.at[n, k], sum_sem.at[n, k], device)

    def reduce_end(n):
        total = sums[n]
        for k in range(len(reduce_peers[n])):
            arrived(sums_in.at[n, k], sum_sem.at[n, k])
            total += sums_in[n, k]
        sums[n + 1] = total

    reduce_start(0)
    rows_s.take(0, 1, 3, 2)
    rows_s.bundle()
    ring_s.take(1, 3)
    ring_s.take(2)
    rows_s.take(1, 1)
    reduce_end(0)
    reduce_start(1)
    ring_s.finish()
    now_columns()
    work(2)
    rows_s.take(1, 3)
    work(len(pending))
    rows_s.take(1, 2)
    work(len(pending))
    reduce_end(1)

    trace_cubic, trace_quartic, spread_sum = (
        jnp.sum(sums[2, n:n + 1], keepdims=True) for n in range(3)
    )
    electrons = F32(rows * 8 // 2)
    factor = (electrons - (4.0 * trace_cubic - 3.0 * trace_quartic)) / (spread_sum + 1e-06)
    for i in range(per):
        for j in range(3):
            three, four = cubic[block(i, j)], quartic[block(i, j)]
            value = 4.0 * three - 3.0 * four + factor * (square[block(i, j)] - 2.0 * three + four)
            blocks[i * 3 + j] = (value * kept(i, j)).astype(BF16)
    for h in range(2):
        for s in range(LIST):
            moved[(2 * r + h) * LIST + s] = blocks[listed[h][s]]
    ring_t = Ring(lambda source: moved.at[pl.ds(2 * source * LIST, 2 * LIST)], end_sem, end_sib_sem)
    ring_t.have(0)

    slots = out.shape[0] // bs

    def number_here(source, carry):
        for h in range(2):
            count = jnp.int32(0)
            for b in range(h * part, (h + 1) * part):
                spots_here[source * tile + b] = jnp.minimum(count, LIST - 1) + (2 * source + h) * LIST
                count = count + keep[source * per + origin(b // 3), c * 3 + b % 3]
        return carry

    lax.fori_loop(0, 8, number_here, 0)

    def place_rows(i, state):
        count, sources = state
        one = jnp.where(owner[i] == r, 1, 0)
        sources = tuple(
            jnp.where((one == 1) & (count == s), i, v) for s, v in enumerate(sources)
        )
        return count + one, sources

    count, sources = lax.fori_loop(
        0, 8 * per, place_rows, (jnp.int32(0), (jnp.int32(0),) * slots)
    )
    ring_t.take(1, 3, 2)
    ring_t.finish()
    for s in range(slots):
        for j in range(3):
            inner = sources[s] % per
            at_place = sources[s] - inner + inner % 2 * (per // 2) + inner // 2
            found = moved[spots_here[at_place * 3 + j]]
            there = (s < count) & (keep[sources[s], c * 3 + j] == 1)
            out[block(s, j)] = jnp.where(there, found, jnp.zeros_like(found))
    for copy in started:
        copy.wait_send()


def packed_step(density, keep_mask, owner_map):
    rows, cols = density.shape
    bs = cols // 3
    per = rows // bs
    dma = pltpu.SemaphoreType.DMA
    return pl.pallas_call(
        packed_kernel,
        out_shape=jax.ShapeDtypeStruct(((per + 2) * bs, cols), BF16),
        in_specs=[
            pl.BlockSpec(memory_space=pltpu.VMEM),
            pl.BlockSpec(memory_space=pltpu.SMEM),
            pl.BlockSpec(memory_space=pltpu.SMEM),
        ],
        out_specs=pl.BlockSpec(memory_space=pltpu.VMEM),
        scratch_shapes=[
            pltpu.VMEM((per * 3, bs, bs), BF16),
            pltpu.VMEM((16, cols, cols), BF16),
            pltpu.VMEM((16, cols, cols), BF16),
            pltpu.VMEM((rows // 2, 4 * cols), BF16),
            pltpu.VMEM((rows, cols), F32),
            pltpu.VMEM((rows, cols), F32),
            pltpu.VMEM((rows, cols), F32),
            pltpu.VMEM((16 * LIST, bs, bs), BF16),
            pltpu.VMEM((3, 8, bs), F32),
            pltpu.VMEM((2, 15, 8, bs), F32),
            pltpu.SMEM((16 * per * 3,), jnp.int32),
            pltpu.SMEM((8 * per * 3,), jnp.int32),
            pltpu.SMEM((32,), jnp.int32),
            pltpu.SMEM((32,), jnp.int32),
            dma((108,)),
            dma((2, 2, 2, 4)),
            dma((2, 4)),
            dma((2, 4)),
            dma((4,)),
            dma((4,)),
            dma((2, 15)),
        ] + [pltpu.VMEM((4 * LIST, bs, bs), BF16)] * 4 + [pltpu.VMEM((BUNDLE, bs, bs), BF16)] * 16,
        compiler_params=pltpu.CompilerParams(
            collective_id=0, has_side_effects=True, vmem_limit_bytes=56 << 20
        ),
    )(density, keep_mask, owner_map)


def step(density, keep_mask, owner_map):
    rows = lax.axis_size("row")
    blocks = keep_mask.shape[0]
    halves = keep_mask.reshape(rows, blocks // rows // 2, 2, 4, 4, 3).sum(axis=(1, 5))
    upper, lower = halves[:, 0], halves[:, 1]
    excess = jnp.maximum(
        jnp.maximum(upper, lower) - LIST,
        jnp.maximum(upper.sum(axis=2, keepdims=True), lower.sum(axis=1, keepdims=True)) - BUNDLE,
    )
    return lax.cond(
        jnp.max(excess) <= 0, packed_step, dense_step, density, keep_mask, owner_map
    ).astype(F32)


def solution(mesh):
    return jax.shard_map(
        step,
        mesh=mesh,
        in_specs=(P("row", "col"), P(), P()),
        out_specs=P("row", "col"),
        check_vma=False,
    )
```

```python
import jax
import jax.numpy as jnp
from jax import lax
from jax.experimental import pallas as pl
from jax.experimental.pallas import tpu as pltpu
from jax.sharding import PartitionSpec as P

MESH = pl.DeviceIdType.MESH
F32 = jnp.float32
BF16 = jnp.bfloat16


def dense_kernel(
    dens, keep, owner, out,
    row_c, row_s, col_c, col_s, square, cubic, quartic, moved, sums, sums_in,
    send_sem, row_sem, col_sem, sib_sem, end_sem, end_sib_sem, sum_sem,
):
    rows, cols = dens.shape
    group = rows // 2
    half = group // 2
    r = lax.axis_index("row")
    c = lax.axis_index("col")
    z, p = r // 2, r % 2
    y, x = c // 4, c % 4
    sign = 1 - 2 * p
    bs = cols // 3
    per = rows // bs
    per_group = per // 2

    def at(dz=0, dp=0, dy=0, dx=0):
        return (
            lax.rem(z + dz + 4, 4) * 2 + lax.rem(p + dp, 2),
            lax.rem(y + dy + 4, 4) * 4 + lax.rem(x + dx + 4, 4),
        )

    sibling = at(dp=1)
    fwd = {"x": at(dx=sign), "y": at(dy=sign), "z": at(dz=sign)}
    bwd = {"x": at(dx=-sign), "y": at(dy=-sign), "z": at(dz=-sign)}
    reduce_peers = (
        [at(dz=k // 2, dp=k % 2) for k in range(1, 8)],
        [at(dx=k) for k in range(1, 4)],
        [at(dy=k) for k in range(1, 4)],
    )

    barrier = pltpu.get_barrier_semaphore()
    for devices in reduce_peers:
        for device in devices:
            pl.semaphore_signal(barrier, inc=1, device_id=device, device_id_type=MESH)

    def block(i, j):
        return (slice(i * bs, (i + 1) * bs), slice(j * bs, (j + 1) * bs))

    def kept(i, j):
        return keep[r * per + i, c * 3 + j].astype(F32)

    for i in range(per):
        for j in range(3):
            value = (dens[block(i, j)] * kept(i, j)).astype(BF16)
            g, inner = divmod(i, per_group)
            row_c[(g, 0) + block(inner, j)] = value
            col_c[(2 * r + g,) + block(inner, j)] = value

    pl.semaphore_wait(barrier, sum(len(devices) for devices in reduce_peers))

    started = []

    def send(src, dst, recv, device):
        copy = pltpu.make_async_remote_copy(
            src_ref=src, dst_ref=dst, send_sem=send_sem.at[len(started)],
            recv_sem=recv, device_id=device, device_id_type=MESH,
        )
        copy.start()
        started.append(copy)

    def arrived(dst, recv):
        pltpu.make_async_remote_copy(
            src_ref=dst, dst_ref=dst, send_sem=send_sem.at[0],
            recv_sem=recv, device_id=sibling, device_id_type=MESH,
        ).wait_recv()

    order = (
        ((1, 0), (3, 0)),
        ((0, 1), (0, 3)),
        ((2, 0),),
        ((1, 1), (3, 1), (1, 3), (3, 3)),
        ((0, 2), (2, 1), (2, 3)),
        ((1, 2), (3, 2)),
        ((2, 2),),
    )
    routes = (("x", "y"), ("y", "x"))

    def slot(h, first, second):
        return 4 * second + first if h == 0 else 4 * first + second

    class Rows:
        def __init__(self, stage, g, row):
            self.stage, self.g, self.row = stage, g, row

        def piece(self, h, place):
            return self.row.at[self.g, place, pl.ds(h * half, half)]

        def pass_on(self, h, first, second, which, direction):
            n = 1 if direction is fwd else 3
            there = ((first + n) % 4, second) if which == 0 else (first, (second + n) % 4)
            goal = slot(h, *there)
            send(
                self.piece(h, slot(h, first, second)), self.piece(h, goal),
                row_sem.at[self.stage, self.g, h, goal], direction[routes[h][which]],
            )

        def turn(self, h, first):
            self.pass_on(h, first, 0, 1, fwd)
            self.pass_on(h, first, 0, 1, bwd)

        def start(self):
            for h in range(2):
                self.pass_on(h, 0, 0, 0, fwd)
                self.pass_on(h, 0, 0, 0, bwd)
            for h in range(2):
                self.turn(h, 0)

        def round(self, number):
            for first, second in order[number]:
                for h in range(2):
                    place = slot(h, first, second)
                    arrived(self.piece(h, place), row_sem.at[self.stage, self.g, h, place])
                    if second == 0:
                        if first == 1:
                            self.pass_on(h, 1, 0, 0, fwd)
                        self.turn(h, first)
                    elif second == 1:
                        self.pass_on(h, first, 1, 1, fwd)

    class Ring:
        def __init__(self, piece, own, shared):
            self.piece, self.own, self.shared = piece, own, shared

        def at(self, core, away, lane_sign):
            return self.piece(lax.rem(z - lane_sign * away + 8, 4) * 2 + core)

        def have(self, away):
            here = self.at(p, away, sign)
            for n, direction in ((1, fwd), (3, bwd)):
                if away == 0 or (away == 1 and n == 1):
                    send(here, here, self.own.at[(away + n) % 4], direction["z"])
            send(here, here, self.shared.at[away], sibling)

        def take(self, *aways):
            for away in aways:
                arrived(self.at(p, away, sign), self.own.at[away])
                self.have(away)

        def finish(self):
            for away in range(4):
                arrived(self.at(1 - p, away, -sign), self.shared.at[away])

    def column_ring(stage, g, col):
        return Ring(lambda source: col.at[2 * source + g], col_sem.at[stage, g], sib_sem.at[stage, g])

    def move_ring(g):
        return Ring(
            lambda source: moved.at[pl.ds(source * per + g * per_group, per_group)],
            end_sem.at[g], end_sib_sem.at[g],
        )

    def multiply(g, row, *pairs):
        here = pl.ds(g * group, group)
        for total, _ in pairs:
            total[here, :] = jnp.zeros((group, cols), F32)

        def one(place, carry):
            behind_y, behind_x = place // 4, place % 4
            k = lax.rem(y - sign * behind_y + 8, 4) * 4 + lax.rem(x - sign * behind_x + 8, 4)
            for total, col in pairs:
                total[here, :] += jnp.dot(row[g, place], col[k], preferred_element_type=F32)
            return carry

        lax.fori_loop(0, 16, one, 0)

    def fold(v):
        return jnp.sum(v.reshape(bs // 8, 8, bs), axis=0)

    totals = [jnp.zeros((8, bs), F32)] * 3

    def make_square(g):
        multiply(g, row_c, (square, col_c))
        for i in range(g * per_group, (g + 1) * per_group):
            for j in range(3):
                value = square[block(i, j)] * kept(i, j)
                square[block(i, j)] = value
                rounded = value.astype(BF16)
                inner = i - g * per_group
                row_s[(g, 0) + block(inner, j)] = rounded
                col_s[(2 * r + g,) + block(inner, j)] = rounded

    def add_sums(g):
        for i in range(g * per_group, (g + 1) * per_group):
            for j in range(3):
                inner = i - g * per_group
                value = square[block(i, j)]
                difference = dens[block(i, j)] * kept(i, j) - value
                wide = row_s[(g, 0) + block(inner, j)].astype(F32)
                one = row_c[(g, 0) + block(inner, j)].astype(F32)
                terms = (wide * one, wide * wide, difference * difference)
                for n, v in enumerate(terms):
                    totals[n] = totals[n] + fold(v)

    def reduce_start(n):
        for k, device in enumerate(reduce_peers[n]):
            send(sums.at[n], sums_in.at[n, k], sum_sem.at[n, k], device)

    def reduce_end(n):
        total = sums[n]
        for k in range(len(reduce_peers[n])):
            arrived(sums_in.at[n, k], sum_sem.at[n, k])
            total += sums_in[n, k]
        sums[n + 1] = total

    def make_result(g):
        multiply(g, row_s, (cubic, col_c), (quartic, col_s))
        trace_cubic, trace_quartic, spread = (
            jnp.sum(sums[3, n], keepdims=True) for n in range(3)
        )
        electrons = F32(rows * 8 // 2)
        factor = (electrons - (4.0 * trace_cubic - 3.0 * trace_quartic)) / (spread + 1e-06)
        for i in range(g * per_group, (g + 1) * per_group):
            for j in range(3):
                three, four = cubic[block(i, j)], quartic[block(i, j)]
                value = 4.0 * three - 3.0 * four + factor * (square[block(i, j)] - 2.0 * three + four)
                moved[r * per + i, :, j * bs:(j + 1) * bs] = (value * kept(i, j)).astype(BF16)

    c0, c1 = (Rows(0, g, row_c) for g in range(2))
    s0, s1 = (Rows(1, g, row_s) for g in range(2))
    zc0, zc1 = (column_ring(0, g, col_c) for g in range(2))
    zs0, zs1 = (column_ring(1, g, col_s) for g in range(2))
    m0, m1 = (move_ring(g) for g in range(2))

    c0.start()
    zc0.have(0)
    zc1.have(0)
    c0.round(0)
    zc0.take(1, 3)
    c0.round(1)
    zc1.take(1, 3)
    c0.round(2)
    zc0.take(2)
    c1.start()
    c0.round(3)
    zc1.take(2)
    zc0.finish()
    zc1.finish()
    c0.round(4)
    c1.round(0)
    c0.round(5)
    c1.round(1)
    c0.round(6)
    make_square(0)
    zs0.have(0)
    c1.round(2)
    s0.start()
    c1.round(3)
    add_sums(0)
    c1.round(4)
    zs0.take(1, 3)
    s0.round(0)
    c1.round(5)
    c1.round(6)
    make_square(1)
    zs1.have(0)
    add_sums(1)
    for n in range(3):
        sums[0, n] = totals[n]
    reduce_start(0)
    zs0.take(2)
    s0.round(1)
    reduce_end(0)
    reduce_start(1)
    s0.round(2)
    zs1.take(1, 3)
    s1.start()
    reduce_end(1)
    reduce_start(2)
    s0.round(3)
    zs1.take(2)
    zs0.finish()
    zs1.finish()
    s0.round(4)
    reduce_end(2)
    s1.round(0)
    s0.round(5)
    s1.round(1)
    s0.round(6)
    make_result(0)
    m0.have(0)
    s1.round(2)
    s1.round(3)
    m0.take(1, 3)
    s1.round(4)
    s1.round(5)
    m0.take(2)
    s1.round(6)
    make_result(1)
    m1.have(0)

    slots = out.shape[0] // bs

    def place(i, state):
        count, sources = state
        mine = jnp.where(owner[i] == r, 1, 0)
        sources = tuple(
            jnp.where((mine == 1) & (count == s), i, v) for s, v in enumerate(sources)
        )
        return count + mine, sources

    count, sources = lax.fori_loop(
        0, 8 * per, place, (jnp.int32(0), (jnp.int32(0),) * slots)
    )
    m1.take(1, 3, 2)
    m0.finish()
    m1.finish()
    for s in range(slots):
        found = moved[sources[s]]
        out[s * bs:(s + 1) * bs, :] = jnp.where(s < count, found, jnp.zeros_like(found))
    for copy in started:
        copy.wait_send()


def dense_step(density, keep_mask, owner_map):
    rows, cols = density.shape
    group, bs = rows // 2, cols // 3
    per = rows // bs
    dma = pltpu.SemaphoreType.DMA
    return pl.pallas_call(
        dense_kernel,
        out_shape=jax.ShapeDtypeStruct(((per + 2) * bs, cols), BF16),
        in_specs=[
            pl.BlockSpec(memory_space=pltpu.VMEM),
            pl.BlockSpec(memory_space=pltpu.SMEM),
            pl.BlockSpec(memory_space=pltpu.SMEM),
        ],
        out_specs=pl.BlockSpec(memory_space=pltpu.VMEM),
        scratch_shapes=[
            pltpu.VMEM((2, 16, group, cols), BF16),
            pltpu.VMEM((2, 16, group, cols), BF16),
            pltpu.VMEM((16, group, cols), BF16),
            pltpu.VMEM((16, group, cols), BF16),
            pltpu.VMEM((rows, cols), F32),
            pltpu.VMEM((rows, cols), F32),
            pltpu.VMEM((rows, cols), F32),
            pltpu.VMEM((8 * per, bs, cols), BF16),
            pltpu.VMEM((4, 3, 8, bs), F32),
            pltpu.VMEM((3, 7, 3, 8, bs), F32),
            dma((180,)),
            dma((2, 2, 2, 16)),
            dma((2, 2, 4)),
            dma((2, 2, 4)),
            dma((2, 4)),
            dma((2, 4)),
            dma((3, 7)),
        ],
        compiler_params=pltpu.CompilerParams(
            collective_id=1, has_side_effects=True, vmem_limit_bytes=56 << 20
        ),
    )(density, keep_mask, owner_map)


LIST = 7
BUNDLE = 18


def packed_kernel(
    dens, keep, owner, out,
    blocks, col_c, col_s, left, square, cubic, quartic, moved, sums, sums_in, spots, spots_here, counts, offsets,
    send_sem, row_sem, col_sem, sib_sem, end_sem, end_sib_sem, sum_sem, *lists,
):
    rows, cols = dens.shape
    bs = cols // 3
    per = rows // bs
    tile = per * 3
    part = tile // 2

    def origin(i):
        return i % (per // 2) * 2 + i // (per // 2)

    list_c, list_s = lists[0:2], lists[2:4]
    bundle_c, bundle_s = (lists[4:8], lists[8:12]), (lists[12:16], lists[16:20])
    r = lax.axis_index("row")
    c = lax.axis_index("col")
    z, p = r // 2, r % 2
    y, x = c // 4, c % 4
    sign = 1 - 2 * p

    def at(dz=0, dp=0, dy=0, dx=0):
        return (
            lax.rem(z + dz + 4, 4) * 2 + lax.rem(p + dp, 2),
            lax.rem(y + dy + 4, 4) * 4 + lax.rem(x + dx + 4, 4),
        )

    sibling = at(dp=1)
    fwd = {"x": at(dx=sign), "y": at(dy=sign), "z": at(dz=sign)}
    bwd = {"x": at(dx=-sign), "y": at(dy=-sign), "z": at(dz=-sign)}
    reduce_peers = (
        [at(dz=k // 2, dp=k % 2) for k in range(1, 8)],
        [at(dy=k // 4, dx=k % 4) for k in range(1, 16)],
    )

    barrier = pltpu.get_barrier_semaphore()
    for devices in reduce_peers:
        for device in devices:
            pl.semaphore_signal(barrier, inc=1, device_id=device, device_id_type=MESH)

    def block(i, j):
        return (slice(i * bs, (i + 1) * bs), slice(j * bs, (j + 1) * bs))

    def kept(i, j):
        return keep[r * per + origin(i), c * 3 + j].astype(F32)

    def col_block(i, j):
        return (2 * r + origin(i) // (per // 2),) + block(origin(i) % (per // 2), j)

    for i in range(per):
        for j in range(3):
            value = (dens[block(origin(i), j)] * kept(i, j)).astype(BF16)
            blocks[i * 3 + j] = value
            col_c[col_block(i, j)] = value

    def find(h):
        count, sources = jnp.int32(0), [jnp.int32(h * part)] * LIST
        for b in range(h * part, (h + 1) * part):
            one = keep[r * per + origin(b // 3), c * 3 + b % 3]
            sources = [
                jnp.where((one == 1) & (count == s), b, v) for s, v in enumerate(sources)
            ]
            count = count + one
        return sources

    listed = [find(0), find(1)]

    def pack(targets):
        for h in range(2):
            for s in range(LIST):
                targets[h][s] = blocks[listed[h][s]]

    pack(list_c)
    pl.semaphore_wait(barrier, sum(len(devices) for devices in reduce_peers))

    started = []

    def send(src, dst, recv, device):
        copy = pltpu.make_async_remote_copy(
            src_ref=src, dst_ref=dst, send_sem=send_sem.at[len(started)],
            recv_sem=recv, device_id=device, device_id_type=MESH,
        )
        copy.start()
        started.append(copy)

    def arrived(dst, recv):
        pltpu.make_async_remote_copy(
            src_ref=dst, dst_ref=dst, send_sem=send_sem.at[0],
            recv_sem=recv, device_id=sibling, device_id_type=MESH,
        ).wait_recv()

    pending = []

    def work(count):
        for _ in range(min(count, len(pending))):
            pending.pop(0)()

    routes = (("x", "y"), ("y", "x"))

    class Rows:
        def __init__(self, stage, lists, bundles, ready):
            self.stage, self.lists, self.bundles, self.ready = stage, lists, bundles, ready

        def piece(self, ring, h, away):
            if ring == 0:
                return self.lists[h].at[pl.ds(away * LIST, LIST)]
            return self.bundles[h][away]

        def have(self, ring, h, away):
            for n, direction in ((1, fwd), (3, bwd)):
                if away == 0 or (away == 1 and n == 1):
                    goal = (away + n) % 4
                    send(
                        self.piece(ring, h, away), self.piece(ring, h, goal),
                        row_sem.at[self.stage, ring, h, goal], direction[routes[h][ring]],
                    )

        def start(self):
            for h in range(2):
                self.have(0, h, 0)

        def take(self, ring, *aways):
            for away in aways:
                for h in range(2):
                    arrived(self.piece(ring, h, away), row_sem.at[self.stage, ring, h, away])
                    self.have(ring, h, away)
                    if ring == 1:
                        self.ready(h, away)

        def bundle(self):
            for h in range(2):
                place = x if h == 0 else y
                starts = [
                    offsets[h * 16 + (4 * y + t if h == 0 else 4 * t + x)] for t in range(4)
                ]
                label = [lax.rem(sign * (place - t) + 8, 4) * LIST for t in range(4)]
                for s in range(BUNDLE):
                    shift = label[0]
                    for t in range(1, 4):
                        shift = jnp.where(s >= starts[t], label[t] - starts[t], shift)
                    source = jnp.minimum(jnp.maximum(s + shift, 0), 4 * LIST - 1)
                    self.bundles[h][0][s] = self.lists[h][source]
                self.have(1, h, 0)
                self.ready(h, 0)

    class Ring:
        def __init__(self, piece, own, shared):
            self.piece, self.own, self.shared = piece, own, shared

        def at(self, core, away, lane_sign):
            return self.piece(lax.rem(z - lane_sign * away + 8, 4) * 2 + core)

        def have(self, away):
            here = self.at(p, away, sign)
            for n, direction in ((1, fwd), (3, bwd)):
                if away == 0 or (away == 1 and n == 1):
                    send(here, here, self.own.at[(away + n) % 4], direction["z"])
            send(here, here, self.shared.at[away], sibling)

        def take(self, *aways):
            for away in aways:
                arrived(self.at(p, away, sign), self.own.at[away])
                self.have(away)

        def finish(self):
            for away in range(4):
                arrived(self.at(1 - p, away, -sign), self.shared.at[away])

    def columns(stage, col):
        return Ring(lambda source: col.at[pl.ds(2 * source, 2)], col_sem.at[stage], sib_sem.at[stage])

    def spread(bundles, h, away):
        behind = lax.rem((y if h == 0 else x) - sign * away + 8, 4)
        bundle = bundles[h][away]
        sources = [4 * behind + t if h == 0 else 4 * t + behind for t in range(4)]
        for t, source in enumerate(sources):
            start = offsets[h * 16 + source]
            for i in range(per // 2):
                for j in range(3):
                    b = (h * per // 2 + i) * 3 + j
                    spot = jnp.minimum(start + spots[source * tile + b], BUNDLE - 1)
                    found = bundle[spot]
                    there = keep[r * per + origin(b // 3), source * 3 + j] == 1
                    left[block(i, 3 * t + j)] = jnp.where(there, found, jnp.zeros_like(found))
        return sources

    fresh = set()

    def add(name, total, h, sources, col):
        here = pl.ds(h * (rows // 2), rows // 2)
        if h == 0:
            right = col[pl.ds(sources[0], 4)].reshape(4 * cols, cols)
        else:
            right = jnp.concatenate([col[source] for source in sources], axis=0)
        term = jnp.dot(left[...], right, preferred_element_type=F32)
        if (name, h) in fresh:
            total[here, :] += term
        else:
            fresh.add((name, h))
            total[here, :] = term

    waiting = []
    columns_ready = []

    def first_product(h, away):
        sources = spread(bundle_c, h, away)
        add("square", square, h, sources, col_c)

    def second_product(h, away):
        sources = spread(bundle_s, h, away)
        add("cubic", cubic, h, sources, col_c)
        add("quartic", quartic, h, sources, col_s)

    def ready_for(product):
        def ready(h, away):
            waiting.append(lambda: product(h, away))
            if columns_ready:
                pending.extend(waiting)
                waiting.clear()
        return ready

    def now_columns():
        columns_ready.append(True)
        pending.extend(waiting)
        waiting.clear()

    rows_c = Rows(0, list_c, bundle_c, ready_for(first_product))
    rows_s = Rows(1, list_s, bundle_s, ready_for(second_product))
    ring_c, ring_s = columns(0, col_c), columns(1, col_s)

    rows_c.start()
    ring_c.have(0)

    def number(source, carry):
        for h in range(2):
            count = jnp.int32(0)
            for b in range(h * part, (h + 1) * part):
                spots[source * tile + b] = count
                count = count + keep[r * per + origin(b // 3), source * 3 + b % 3]
            counts[2 * source + h] = count
        return carry

    lax.fori_loop(0, 16, number, 0)
    for h in range(2):
        for i in range(4):
            start = jnp.int32(0)
            for t in range(4):
                source = 4 * i + t if h == 0 else 4 * t + i
                offsets[h * 16 + source] = start
                start = start + counts[2 * source + h]

    rows_c.take(0, 1, 3, 2)
    rows_c.bundle()
    ring_c.take(1, 3)
    ring_c.take(2)
    rows_c.take(1, 1)
    ring_c.finish()
    now_columns()
    work(3)
    rows_c.take(1, 3)
    work(len(pending))
    rows_c.take(1, 2)
    work(len(pending))
    columns_ready.clear()

    for i in range(per):
        for j in range(3):
            value = square[block(i, j)] * kept(i, j)
            square[block(i, j)] = value
            rounded = value.astype(BF16)
            col_s[col_block(i, j)] = rounded
            blocks[i * 3 + j] = rounded
    pack(list_s)
    rows_s.start()
    ring_s.have(0)

    def fold(v):
        return jnp.sum(v.reshape(bs // 8, 8, bs), axis=0)

    totals = [jnp.zeros((8, bs), F32)] * 3
    for i in range(per):
        for j in range(3):
            value = square[block(i, j)]
            difference = dens[block(origin(i), j)] * kept(i, j) - value
            wide = blocks[i * 3 + j].astype(F32)
            one = col_c[col_block(i, j)].astype(F32)
            terms = (wide * one, wide * wide, difference * difference)
            totals = [t + fold(v) for t, v in zip(totals, terms, strict=True)]
    sums[0] = jnp.zeros((8, bs), F32)
    for n in range(3):
        sums[0, n:n + 1] = jnp.sum(totals[n], axis=0, keepdims=True)

    def reduce_start(n):
        for k, device in enumerate(reduce_peers[n]):
            send(sums.at[n], sums_in.at[n, k], sum_sem.at[n, k], device)

    def reduce_end(n):
        total = sums[n]
        for k in range(len(reduce_peers[n])):
            arrived(sums_in.at[n, k], sum_sem.at[n, k])
            total += sums_in[n, k]
        sums[n + 1] = total

    reduce_start(0)
    rows_s.take(0, 1, 3, 2)
    rows_s.bundle()
    ring_s.take(1, 3)
    ring_s.take(2)
    rows_s.take(1, 1)
    reduce_end(0)
    reduce_start(1)
    ring_s.finish()
    now_columns()
    work(2)
    rows_s.take(1, 3)
    work(len(pending))
    rows_s.take(1, 2)
    reduce_end(1)
    trace_cubic, trace_quartic, spread_sum = (
        jnp.sum(sums[2, n:n + 1], keepdims=True) for n in range(3)
    )
    electrons = F32(rows * 8 // 2)
    factor = (electrons - (4.0 * trace_cubic - 3.0 * trace_quartic)) / (spread_sum + 1e-06)

    def move_ring(h):
        return Ring(
            lambda source: moved.at[pl.ds((2 * source + h) * LIST, LIST)],
            end_sem.at[h], end_sib_sem.at[h],
        )

    rings_t = [move_ring(0), move_ring(1)]
    for h in range(2):
        work(1)
        for i in range(h * per // 2, (h + 1) * per // 2):
            for j in range(3):
                three, four = cubic[block(i, j)], quartic[block(i, j)]
                value = 4.0 * three - 3.0 * four + factor * (square[block(i, j)] - 2.0 * three + four)
                blocks[i * 3 + j] = (value * kept(i, j)).astype(BF16)
        for s in range(LIST):
            moved[(2 * r + h) * LIST + s] = blocks[listed[h][s]]
        rings_t[h].have(0)

    slots = out.shape[0] // bs

    def number_here(source, carry):
        for h in range(2):
            count = jnp.int32(0)
            for b in range(h * part, (h + 1) * part):
                spots_here[source * tile + b] = jnp.minimum(count, LIST - 1) + (2 * source + h) * LIST
                count = count + keep[source * per + origin(b // 3), c * 3 + b % 3]
        return carry

    lax.fori_loop(0, 8, number_here, 0)

    def place_rows(i, state):
        count, sources = state
        one = jnp.where(owner[i] == r, 1, 0)
        sources = tuple(
            jnp.where((one == 1) & (count == s), i, v) for s, v in enumerate(sources)
        )
        return count + one, sources

    count, sources = lax.fori_loop(
        0, 8 * per, place_rows, (jnp.int32(0), (jnp.int32(0),) * slots)
    )
    for away in (1, 3, 2):
        for ring in rings_t:
            ring.take(away)
    for ring in rings_t:
        ring.finish()
    for s in range(slots):
        for j in range(3):
            inner = sources[s] % per
            at_place = sources[s] - inner + inner % 2 * (per // 2) + inner // 2
            found = moved[spots_here[at_place * 3 + j]]
            there = (s < count) & (keep[sources[s], c * 3 + j] == 1)
            out[block(s, j)] = jnp.where(there, found, jnp.zeros_like(found))
    for copy in started:
        copy.wait_send()


def packed_step(density, keep_mask, owner_map):
    rows, cols = density.shape
    bs = cols // 3
    per = rows // bs
    dma = pltpu.SemaphoreType.DMA
    return pl.pallas_call(
        packed_kernel,
        out_shape=jax.ShapeDtypeStruct(((per + 2) * bs, cols), BF16),
        in_specs=[
            pl.BlockSpec(memory_space=pltpu.VMEM),
            pl.BlockSpec(memory_space=pltpu.SMEM),
            pl.BlockSpec(memory_space=pltpu.SMEM),
        ],
        out_specs=pl.BlockSpec(memory_space=pltpu.VMEM),
        scratch_shapes=[
            pltpu.VMEM((per * 3, bs, bs), BF16),
            pltpu.VMEM((16, cols, cols), BF16),
            pltpu.VMEM((16, cols, cols), BF16),
            pltpu.VMEM((rows // 2, 4 * cols), BF16),
            pltpu.VMEM((rows, cols), F32),
            pltpu.VMEM((rows, cols), F32),
            pltpu.VMEM((rows, cols), F32),
            pltpu.VMEM((16 * LIST, bs, bs), BF16),
            pltpu.VMEM((3, 8, bs), F32),
            pltpu.VMEM((2, 15, 8, bs), F32),
            pltpu.SMEM((16 * per * 3,), jnp.int32),
            pltpu.SMEM((8 * per * 3,), jnp.int32),
            pltpu.SMEM((32,), jnp.int32),
            pltpu.SMEM((32,), jnp.int32),
            dma((108,)),
            dma((2, 2, 2, 4)),
            dma((2, 4)),
            dma((2, 4)),
            dma((2, 4)),
            dma((2, 4)),
            dma((2, 15)),
        ] + [pltpu.VMEM((4 * LIST, bs, bs), BF16)] * 4 + [pltpu.VMEM((BUNDLE, bs, bs), BF16)] * 16,
        compiler_params=pltpu.CompilerParams(
            collective_id=0, has_side_effects=True, vmem_limit_bytes=56 << 20
        ),
    )(density, keep_mask, owner_map)


def step(density, keep_mask, owner_map):
    rows = lax.axis_size("row")
    blocks = keep_mask.shape[0]
    halves = keep_mask.reshape(rows, blocks // rows // 2, 2, 4, 4, 3).sum(axis=(1, 5))
    upper, lower = halves[:, 0], halves[:, 1]
    excess = jnp.maximum(
        jnp.maximum(upper, lower) - LIST,
        jnp.maximum(upper.sum(axis=2, keepdims=True), lower.sum(axis=1, keepdims=True)) - BUNDLE,
    )
    return lax.cond(
        jnp.max(excess) <= 0, packed_step, dense_step, density, keep_mask, owner_map
    ).astype(F32)


def solution(mesh):
    return jax.shard_map(
        step,
        mesh=mesh,
        in_specs=(P("row", "col"), P(), P()),
        out_specs=P("row", "col"),
        check_vma=False,
    )
```
